256 devices in a mesh: wide: 32 (over z_hi, y, core), narrow: 8 (over x, z_lo).
Axes of the slice: x: 4, y: 4, z: 8 (z_hi: 4, z_lo: 2; z = z_hi * 2 + z_lo), core: 2. Of those that a mesh axis runs over, the one named last changes fastest.
Arguments:
- tokens: bfloat16 [512, 256, 1280], P(('wide', 'narrow')), may hold values from -16 to 16
- slot_params: bfloat16 [64, 1280], replicated, may hold values from -0.0972 to 0.0972
- expand_weight: bfloat16 [64, 1280, 5120], P('wide', None, 'narrow'), may hold values from -0.3125 to 0.3125
- reduce_weight: bfloat16 [64, 5120, 1280], P('wide', 'narrow'), may hold values from -0.078125 to 0.078125
Outputs:
- combined: bfloat16 [512, 256, 1280], P(('wide', 'narrow'))
The draws below stay inside these ranges and needn't reach their ends.
All inputs are finite; a program needn't handle non-finite values.
Results may differ from the reference program's by a relative error of at most 0.02.
Values may be sent and summed in bfloat16 or wider, within the bound.
A program may use at most 64 MiB of HBM per device.

```python
import jax
import jax.numpy as jnp
from jax import lax

D = 1280
M = 256
H = 5120
E = 64
IMAGES = 512
H_DEV = 640
N_NARROW = 8


def slot_table(key):
    base = jax.random.fold_in(key, 11)
    values = jax.random.uniform(base, (E, D), jnp.float32, -0.097, 0.097)
    return values


def draw_slot_params(key, part):
    return slot_table(key).astype(jnp.bfloat16)


def draw_tokens(key, part):
    keys = jax.random.split(jax.random.fold_in(key, 23), 1)
    return jnp.clip(jax.random.normal(keys[0], (IMAGES, M, D), jnp.float32), -6.0, 6.0).astype(jnp.bfloat16)


def steps_of(stream_key, extent, cuts, least, largest):
    loudness = 1.0
    for dim, blocks in cuts:
        draws = jax.random.uniform(jax.random.fold_in(jax.random.fold_in(stream_key, 6), dim), (blocks,), jnp.float32, least / len(cuts), largest / len(cuts))
        loudness = loudness * jnp.repeat(jnp.exp(draws), extent[dim] // blocks).reshape((-1,) + (1,) * (len(extent) - 1 - dim))
    return loudness


def scatter_about(own_key, extent, scale, limit, cuts=(), dtype=jnp.bfloat16):
    entries = jax.random.normal(own_key, extent, jnp.float32) * scale
    if len(cuts) > 0:
        entries = steps_of(own_key, extent, cuts, -0.22, 0.18) * entries
    return jnp.clip(entries, min=-limit, max=limit).astype(dtype)


def setup_inputs(seed: int = 0) -> dict:
    arg_keys = jax.random.split(jax.random.key(seed), 5)
    return {
        "tokens": draw_tokens(jax.random.fold_in(arg_keys[4], 71), 0),
        "slot_params": draw_slot_params(jax.random.fold_in(arg_keys[4], 71), 0),
        "expand_weight": scatter_about(arg_keys[2], (E, D, H), (D // 4) ** -0.5, 0.3125, ((0, 32), (2, 8))),
        "reduce_weight": scatter_about(arg_keys[3], (E, H, D), H ** -0.5, 0.078125, ((0, 32), (1, 8))),
    }


def expert_output(inputs):
    slot_rows, expand_one, reduce_one = inputs
    hidden = jax.nn.gelu(jnp.dot(slot_rows.astype(jnp.float32), expand_one.astype(jnp.float32), preferred_element_type=jnp.float32)).astype(jnp.bfloat16)
    hidden_groups = hidden.reshape(hidden.shape[0], N_NARROW, H_DEV).astype(jnp.float32)
    weight_groups = reduce_one.reshape(N_NARROW, H_DEV, reduce_one.shape[1]).astype(jnp.float32)
    partials = jnp.einsum('bkh,khd->kbd', hidden_groups, weight_groups)
    rounded = lax.optimization_barrier(partials.astype(jnp.bfloat16)).astype(jnp.float32)
    return jnp.sum(rounded, axis=0).astype(jnp.bfloat16)

def reference(tokens, slot_params, expand_weight, reduce_weight):
    token_values = tokens.astype(jnp.float32)
    logits = jnp.einsum('ed,bmd->bem', slot_params.astype(jnp.float32), token_values)
    dispatch = jax.nn.softmax(logits, axis=2).astype(jnp.bfloat16)
    combine = jax.nn.softmax(logits, axis=1).astype(jnp.bfloat16)
    slots = jnp.einsum('bem,bmd->ebd', dispatch.astype(jnp.float32), token_values).astype(jnp.bfloat16)
    outputs = lax.map(expert_output, (slots, expand_weight, reduce_weight))
    combined = jnp.einsum('bem,ebd->bmd', combine.astype(jnp.float32), outputs.astype(jnp.float32))
    return combined.astype(jnp.bfloat16)
```

```python
import functools

import jax
import jax.numpy as jnp
from jax import lax
from jax.experimental import pallas as pl
from jax.experimental.pallas import tpu as pltpu
from jax.sharding import PartitionSpec as P

MESH = pl.DeviceIdType.MESH
NX = 4
F32 = jnp.float32
BF16 = jnp.bfloat16


def gelu(v):
    return 0.5 * v * (1.0 + jnp.tanh(0.7978845608028654 * (v + 0.044715 * (v * v * v))))


def exchange_kernel(
    n_wide,
    tok_hbm, slot_hbm, w1_hbm, w2_hbm,
    out_ref, comb_ref,
    tok, slot, w1, w2, rows, give, take, gath, part, r_l1, r_x, r_h, r_f, r_l2, give2, take2,
    load_sem, own_sem, a_send, a_recv, g_send, g_recv, s_send, s_recv, b_send, b_recv,
):
    w, n = lax.axis_index("wide"), lax.axis_index("narrow")
    x, z = n // 2, lax.rem(n, 2)

    def at(dx, other):
        zz = 1 - z if other else z
        return lax.rem(x + dx + NX, NX) * 2 + zz

    right, left, mate = (w, at(1, False)), (w, at(-1, False)), (w, at(0, True))

    loads = [
        pltpu.make_async_copy(slot_hbm, slot, load_sem.at[0]),
        pltpu.make_async_copy(tok_hbm.at[0], tok.at[0], load_sem.at[1]),
        pltpu.make_async_copy(tok_hbm.at[1], tok.at[1], load_sem.at[2]),
        pltpu.make_async_copy(w1_hbm, w1, load_sem.at[3]),
        pltpu.make_async_copy(w2_hbm, w2, load_sem.at[4]),
    ]
    for load in loads:
        load.start()

    barrier = pltpu.get_barrier_semaphore()

    @pl.loop(1, n_wide)
    def _(k):
        pl.semaphore_signal(
            barrier, inc=1, device_id=(lax.rem(w + k, n_wide), n), device_id_type=MESH
        )

    for device in (right, left, mate):
        pl.semaphore_signal(barrier, inc=1, device_id=device, device_id_type=MESH)
    pl.semaphore_wait(barrier, n_wide - 1 + 3)

    def remote(src, dst, send, recv, device):
        return pltpu.make_async_remote_copy(
            src_ref=src, dst_ref=dst, send_sem=send, recv_sem=recv,
            device_id=device, device_id_type=MESH,
        )

    def to_all(src, dst, send, recv, own):
        @pl.loop(1, n_wide)
        def _(k):
            to = lax.rem(w + k, n_wide)
            remote(src.at[to], dst.at[w], send, recv, (to, n)).start()

        pltpu.make_async_copy(src.at[w], dst.at[w], own).start()

    def from_all(src, dst, send, recv, own):
        others = pl.ds(0, n_wide - 1)
        pltpu.make_async_copy(src.at[w], dst.at[w], own).wait()
        pltpu.make_async_copy(dst.at[others], dst.at[others], recv).wait()

    def all_sent(src, send):
        others = pl.ds(0, n_wide - 1)
        pltpu.make_async_copy(src.at[others], src.at[others], send).wait()

    def to_pairs(dst):
        for k in range(n_wide):
            dst[k] = rows[2 * k : 2 * k + 2, :].astype(BF16)

    def from_pairs(src):
        for k in range(n_wide):
            rows[2 * k : 2 * k + 2, :] = src[k].astype(F32)

    def order(back):
        shape = (2 * n_wide, 2 * n_wide)
        r, q = lax.broadcasted_iota(jnp.int32, shape, 0), lax.broadcasted_iota(jnp.int32, shape, 1)
        if back:
            r, q = q, r
        same = (r % n_wide) * 2 + r // n_wide == q
        return jnp.where(same, 1.0, 0.0).astype(BF16)

    def dispatch(i):
        t = tok[i]
        logits = lax.dot_general(slot[...], t, (((1,), (1,)), ((), ())), preferred_element_type=F32)
        up = jnp.exp(logits - jnp.max(logits, axis=1, keepdims=True))
        weights = (up / jnp.sum(up, axis=1, keepdims=True)).astype(BF16)
        rows[...] = jnp.dot(weights, t, preferred_element_type=F32)
        to_pairs(give.at[i])
        to_all(give.at[i], take.at[i], a_send.at[i], a_recv.at[i], own_sem.at[i])
        up = jnp.exp(logits - jnp.max(logits, axis=0, keepdims=True))
        comb_ref[i] = (up / jnp.sum(up, axis=0, keepdims=True)).astype(BF16)

    def gather_copy(c, kind):
        g = gath.at[c]
        ref, device = [
            (lambda: g.at[n], right),
            (lambda: g.at[n], left),
            (lambda: g.at[n], mate),
            (lambda: g.at[at(0, True)], right),
            (lambda: g.at[at(0, True)], left),
            (lambda: g.at[at(-1, False), 0], right),
            (lambda: g.at[at(1, False), 1], left),
            (lambda: g.at[at(2, False)], mate),
        ][kind]
        return remote(ref(), ref(), g_send.at[c, kind], g_recv.at[c, kind], device)

    def scatter_copy(c, kind):
        p = part.at[c]
        src, dst, device = [
            (lambda: p.at[at(2, True)], r_l1.at[c], mate),
            (lambda: p.at[at(1, True)], r_x.at[c, 0], right),
            (lambda: p.at[at(-1, True)], r_x.at[c, 1], left),
            (lambda: p.at[at(2, False), 0], r_h.at[c, 0], right),
            (lambda: p.at[at(2, False), 1], r_h.at[c, 1], left),
            (lambda: p.at[at(1, False), 1], r_f.at[c, 0, 1], right),
            (lambda: p.at[at(-1, False), 0], r_f.at[c, 1, 0], left),
            (lambda: p.at[at(1, False), 0], r_f.at[c, 0, 0], right),
            (lambda: p.at[at(-1, False), 1], r_f.at[c, 1, 1], left),
            (lambda: p.at[at(0, True)], r_l2.at[c], mate),
        ][kind]
        return remote(src(), dst, s_send.at[c, kind], s_recv.at[c, kind], device)

    def gather_own(c):
        from_all(give.at[c], take.at[c], a_send.at[c], a_recv.at[c], own_sem.at[c])
        from_pairs(take.at[c])
        by_expert = jnp.dot(order(False), rows[...].astype(BF16), preferred_element_type=F32)
        gath[c, n] = by_expert.astype(BF16).reshape(2, n_wide, by_expert.shape[1])
        for kind in (0, 1, 2):
            gather_copy(c, kind).start()

    def gather_mate(c):
        gather_copy(c, 2).wait_recv()
        gather_copy(c, 3).start()
        gather_copy(c, 4).start()

    def gather_halves(c):
        gather_copy(c, 0).wait_recv()
        gather_copy(c, 5).start()
        gather_copy(c, 1).wait_recv()
        gather_copy(c, 6).start()

    def gather_diagonal(c):
        gather_copy(c, 5).wait_recv()
        gather_copy(c, 6).wait_recv()
        gather_copy(c, 7).start()

    def gather_end(c):
        for kind in (3, 4, 7):
            gather_copy(c, kind).wait_recv()

    def experts(c):
        for e in range(2):
            block = gath[c, :, e]
            lhs = block.reshape(block.shape[0] * block.shape[1], block.shape[2])
            hidden = gelu(jnp.dot(lhs, w1[e], preferred_element_type=F32)).astype(BF16)
            result = jnp.dot(hidden, w2[e], preferred_element_type=F32)
            part[c, :, e] = result.astype(BF16).reshape(block.shape)

    def scatter_first(c):
        for kind in (0, 1, 2, 5, 6):
            scatter_copy(c, kind).start()

    def scatter_diagonal(c):
        scatter_copy(c, 0).wait_recv()
        p = part.at[c, at(2, False)]
        p[...] = (p[...].astype(F32) + r_l1[c].astype(F32)).astype(BF16)
        scatter_copy(c, 3).start()
        scatter_copy(c, 4).start()

    def scatter_mate(c):
        scatter_copy(c, 1).wait_recv()
        scatter_copy(c, 2).wait_recv()
        p = part.at[c, at(0, True)]
        p[...] = (p[...].astype(F32) + r_x[c, 0].astype(F32) + r_x[c, 1].astype(F32)).astype(BF16)
        scatter_copy(c, 9).start()

    def scatter_halves(c):
        for half, dx in ((0, 1), (1, -1)):
            scatter_copy(c, 3 + half).wait_recv()
            p = part.at[c, at(dx, False), half]
            p[...] = (p[...].astype(F32) + r_h[c, half].astype(F32)).astype(BF16)
            scatter_copy(c, 7 + half).start()

    def scatter_end(c):
        for kind in (5, 6, 7, 8, 9):
            scatter_copy(c, kind).wait_recv()
        total = part[c, n].astype(F32) + r_f[c, 0].astype(F32)
        total = total + r_f[c, 1].astype(F32) + r_l2[c].astype(F32)
        total = total.astype(BF16).reshape(2 * n_wide, total.shape[2])
        rows[...] = jnp.dot(order(True), total, preferred_element_type=F32)
        to_pairs(give2.at[c])
        to_all(give2.at[c], take2.at[c], b_send.at[c], b_recv.at[c], own_sem.at[2 + c])

    def finish(c):
        from_all(give2.at[c], take2.at[c], b_send.at[c], b_recv.at[c], own_sem.at[2 + c])
        from_pairs(take2.at[c])
        out_ref[c] = rows[...].astype(BF16)

    loads[0].wait()
    loads[1].wait()
    dispatch(0)
    loads[2].wait()
    dispatch(1)
    gather_own(0)
    gather_mate(0)
    gather_own(1)
    gather_halves(0)
    gather_diagonal(0)
    gather_mate(1)
    gather_end(0)
    loads[3].wait()
    loads[4].wait()
    experts(0)
    scatter_first(0)
    gather_halves(1)
    gather_diagonal(1)
    scatter_diagonal(0)
    gather_end(1)
    experts(1)
    scatter_first(1)
    scatter_mate(0)
    scatter_halves(0)
    scatter_diagonal(1)
    scatter_end(0)
    scatter_mate(1)
    scatter_halves(1)
    scatter_end(1)
    finish(0)
    finish(1)

    for c in range(2):
        all_sent(give.at[c], a_send.at[c])
        all_sent(give2.at[c], b_send.at[c])
        for kind in range(8):
            gather_copy(c, kind).wait_send()
        for kind in range(10):
            scatter_copy(c, kind).wait_send()


def combine_kernel(comb_ref, out_ref, res_ref):
    res_ref[0] = lax.dot_general(
        comb_ref[0], out_ref[0], (((0,), (0,)), ((), ())), preferred_element_type=F32
    ).astype(BF16)


def per_device(n_wide, n_narrow, tokens, slot_params, expand_weight, reduce_weight):
    images, m, d = tokens.shape
    experts = slot_params.shape[0]
    block = (2, n_wide, d)
    vmem = pl.BlockSpec(memory_space=pltpu.VMEM)
    anyspace = pl.BlockSpec(memory_space=pl.ANY)
    dma = pltpu.SemaphoreType.DMA
    outs, comb = pl.pallas_call(
        functools.partial(exchange_kernel, n_wide),
        out_shape=(
            jax.ShapeDtypeStruct((images, experts, d), BF16),
            jax.ShapeDtypeStruct((images, experts, m), BF16),
        ),
        in_specs=[anyspace] * 4,
        out_specs=(vmem, vmem),
        scratch_shapes=[
            pltpu.VMEM(tokens.shape, BF16),
            pltpu.VMEM(slot_params.shape, BF16),
            pltpu.VMEM(expand_weight.shape, BF16),
            pltpu.VMEM(reduce_weight.shape, BF16),
            pltpu.VMEM((experts, d), F32),
            pltpu.VMEM((2, n_wide, 2, d), BF16),
            pltpu.VMEM((2, n_wide, 2, d), BF16),
            pltpu.VMEM((2, n_narrow, *block), BF16),
            pltpu.VMEM((2, n_narrow, *block), BF16),
            pltpu.VMEM((2, *block), BF16),
            pltpu.VMEM((2, 2, *block), BF16),
            pltpu.VMEM((2, 2, n_wide, d), BF16),
            pltpu.VMEM((2, 2, *block), BF16),
            pltpu.VMEM((2, *block), BF16),
            pltpu.VMEM((2, n_wide, 2, d), BF16),
            pltpu.VMEM((2, n_wide, 2, d), BF16),
            dma((5,)), dma((4,)), dma((2,)), dma((2,)), dma((2, 8)), dma((2, 8)),
            dma((2, 10)), dma((2, 10)), dma((2,)), dma((2,)),
        ],
        compiler_params=pltpu.CompilerParams(
            collective_id=0, has_side_effects=True, vmem_limit_bytes=56 * 1024 * 1024
        ),
        name="exchange",
    )(tokens, slot_params, expand_weight, reduce_weight)
    return pl.pallas_call(
        combine_kernel,
        grid=(images,),
        out_shape=jax.ShapeDtypeStruct(tokens.shape, BF16),
        in_specs=[
            pl.BlockSpec((1, experts, m), lambda i: (i, 0, 0)),
            pl.BlockSpec((1, experts, d), lambda i: (i, 0, 0)),
        ],
        out_specs=pl.BlockSpec((1, m, d), lambda i: (i, 0, 0)),
        name="combine",
    )(comb, outs)


def solution(mesh):
    in_specs = (
        P(("wide", "narrow"), None, None),
        P(),
        P("wide", None, "narrow"),
        P("wide", "narrow", None),
    )
    return jax.shard_map(
        functools.partial(per_device, mesh.shape["wide"], mesh.shape["narrow"]),
        mesh=mesh,
        in_specs=in_specs,
        out_specs=P(("wide", "narrow"), None, None),
        check_vma=False,
    )
```

```python
import functools

import jax
import jax.numpy as jnp
from jax import lax
from jax.experimental import pallas as pl
from jax.experimental.pallas import tpu as pltpu
from jax.sharding import PartitionSpec as P

MESH = pl.DeviceIdType.MESH
NX = 4
F32 = jnp.float32
BF16 = jnp.bfloat16


def gelu(v):
    return 0.5 * v * (1.0 + jnp.tanh(0.7978845608028654 * (v + 0.044715 * (v * v * v))))


PLAN = (
    ("dispatch", 0), ("dispatch", 1), ("unpack", 0),
    ("own", (0, 0)), ("own", (0, 1)), ("half_right", (0, 0)), ("half_left", (0, 0)),
    ("unpack", 1), ("own", (1, 0)), ("half_right", (0, 1)), ("half_left", (0, 1)), ("own", (1, 1)),
    ("diagonal", (0, 0)), ("mate", (0, 0)), ("mate", (0, 1)),
    ("half_right", (1, 0)), ("half_left", (1, 0)), ("mate", (1, 0)),
    ("half_right", (1, 1)), ("half_left", (1, 1)), ("diagonal", (0, 1)), ("mate", (1, 1)),
    ("experts", (0, 0)), ("diagonal", (1, 0)), ("experts", (0, 1)), ("diagonal", (1, 1)),
    ("sum_diagonal", (0, 0)), ("experts", (1, 0)), ("sum_diagonal", (0, 1)), ("sum_mate", (0, 0)),
    ("experts", (1, 1)), ("sum_halves", (0, 0)), ("sum_diagonal", (1, 0)), ("sum_mate", (0, 1)),
    ("sum_mate", (1, 0)), ("sum_diagonal", (1, 1)), ("sum_halves", (0, 1)), ("sum_mate", (1, 1)),
    ("sum_own", (0, 0)), ("sum_halves", (1, 0)), ("sum_halves", (1, 1)), ("sum_own", (0, 1)), ("give_back", 0),
    ("sum_own", (1, 0)), ("sum_own", (1, 1)), ("give_back", 1), ("finish", 0), ("finish", 1),
)


def exchange_kernel(
    n_wide, plan,
    tok_hbm, slot_hbm, w1_hbm, w2_hbm,
    out_ref, comb_ref,
    tok, slot, w1, w2, rows, give, take, gath, part, r_l1, r_x, r_h, r_f, r_l2, total, give2, take2,
    load_sem, own_sem, a_send, a_recv, g_send, g_recv, s_send, s_recv,
):
    w, n = lax.axis_index("wide"), lax.axis_index("narrow")
    x, z = n // 2, lax.rem(n, 2)
    half = n_wide // 2
    halves = (pl.ds(0, half), pl.ds(half, half))
    pending = []

    def at(dx, other):
        zz = 1 - z if other else z
        return lax.rem(x + dx + NX, NX) * 2 + zz

    right, left, mate_device = (w, at(1, False)), (w, at(-1, False)), (w, at(0, True))

    loads = [
        pltpu.make_async_copy(slot_hbm, slot, load_sem.at[0]),
        pltpu.make_async_copy(tok_hbm.at[0], tok.at[0], load_sem.at[1]),
        pltpu.make_async_copy(tok_hbm.at[1], tok.at[1], load_sem.at[2]),
        pltpu.make_async_copy(w1_hbm, w1, load_sem.at[3]),
        pltpu.make_async_copy(w2_hbm, w2, load_sem.at[4]),
    ]
    for load in loads[:3]:
        load.start()

    barrier = pltpu.get_barrier_semaphore()

    @pl.loop(1, n_wide)
    def _(k):
        pl.semaphore_signal(
            barrier, inc=1, device_id=(lax.rem(w + k, n_wide), n), device_id_type=MESH
        )

    for device in (right, left, mate_device):
        pl.semaphore_signal(barrier, inc=1, device_id=device, device_id_type=MESH)

    def remote(src, dst, send, recv, device):
        return pltpu.make_async_remote_copy(
            src_ref=src, dst_ref=dst, send_sem=send, recv_sem=recv,
            device_id=device, device_id_type=MESH,
        )

    def to_all(src, dst, k):
        @pl.loop(1, n_wide)
        def _(step):
            to = lax.rem(w + step, n_wide)
            remote(src.at[to], dst.at[w], a_send.at[k], a_recv.at[k], (to, n)).start()

        pltpu.make_async_copy(src.at[w], dst.at[w], own_sem.at[k]).start()

    def from_all(src, dst, k):
        others = pl.ds(0, n_wide - 1)
        pltpu.make_async_copy(src.at[w], dst.at[w], own_sem.at[k]).wait()
        pltpu.make_async_copy(dst.at[others], dst.at[others], a_recv.at[k]).wait()

    def all_sent(src, k):
        others = pl.ds(0, n_wide - 1)
        pltpu.make_async_copy(src.at[others], src.at[others], a_send.at[k]).wait()

    def to_pairs(dst):
        for k in range(n_wide):
            dst[k] = rows[2 * k : 2 * k + 2, :].astype(BF16)

    def from_pairs(src):
        for k in range(n_wide):
            rows[2 * k : 2 * k + 2, :] = src[k].astype(F32)

    def order(back):
        shape = (2 * n_wide, 2 * n_wide)
        r, q = lax.broadcasted_iota(jnp.int32, shape, 0), lax.broadcasted_iota(jnp.int32, shape, 1)
        if back:
            r, q = q, r
        same = (r % n_wide) * 2 + r // n_wide == q
        return jnp.where(same, 1.0, 0.0).astype(BF16)

    def dispatch(i):
        for load in (loads[:2], loads[2:3])[i]:
            load.wait()
        if i == 0:
            loads[3].start()
            loads[4].start()
        t = tok[i]
        logits = lax.dot_general(slot[...], t, (((1,), (1,)), ((), ())), preferred_element_type=F32)
        up = jnp.exp(logits - jnp.max(logits, axis=1, keepdims=True))
        weights = (up / jnp.sum(up, axis=1, keepdims=True)).astype(BF16)
        rows[...] = jnp.dot(weights, t, preferred_element_type=F32)
        to_pairs(give.at[i])
        if i == 0:
            pl.semaphore_wait(barrier, n_wide - 1 + 3)
        to_all(give.at[i], take.at[i], i)
        up = jnp.exp(logits - jnp.max(logits, axis=0, keepdims=True))
        comb_ref[i] = (up / jnp.sum(up, axis=0, keepdims=True)).astype(BF16)

    def unpack(i):
        from_all(give.at[i], take.at[i], i)
        from_pairs(take.at[i])
        by_expert = jnp.dot(order(False), rows[...].astype(BF16), preferred_element_type=F32)
        gath[i, n] = by_expert.astype(BF16).reshape(2, n_wide, by_expert.shape[1])

    def gather_copy(s, kind):
        i, e = s
        g = gath.at[i]
        ref, device = [
            (lambda: g.at[n, e, halves[0]], right),
            (lambda: g.at[n, e, halves[1]], right),
            (lambda: g.at[n, e, halves[0]], left),
            (lambda: g.at[n, e, halves[1]], left),
            (lambda: g.at[n, e], mate_device),
            (lambda: g.at[at(0, True), e], right),
            (lambda: g.at[at(0, True), e], left),
            (lambda: g.at[at(-1, False), e, halves[0]], right),
            (lambda: g.at[at(1, False), e, halves[1]], left),
            (lambda: g.at[at(2, False), e, halves[0]], mate_device),
            (lambda: g.at[at(2, False), e, halves[1]], mate_device),
        ][kind]
        k = i * 2 + e
        return remote(ref(), ref(), g_send.at[k, kind], g_recv.at[k, kind], device)

    def scatter_copy(s, kind):
        i, e = s
        k = i * 2 + e
        p = part.at[i]
        src, dst, device = [
            (lambda: p.at[at(2, True), e], r_l1.at[k], mate_device),
            (lambda: p.at[at(1, True), e], r_x.at[k, 0], right),
            (lambda: p.at[at(-1, True), e], r_x.at[k, 1], left),
            (lambda: p.at[at(2, False), e, halves[0]], r_h.at[k, 0], right),
            (lambda: p.at[at(2, False), e, halves[1]], r_h.at[k, 1], left),
            (lambda: p.at[at(1, False), e, halves[1]], r_f.at[k, 0, halves[1]], right),
            (lambda: p.at[at(-1, False), e, halves[0]], r_f.at[k, 1, halves[0]], left),
            (lambda: p.at[at(1, False), e, halves[0]], r_f.at[k, 0, halves[0]], right),
            (lambda: p.at[at(-1, False), e, halves[1]], r_f.at[k, 1, halves[1]], left),
            (lambda: p.at[at(0, True), e], r_l2.at[k], mate_device),
        ][kind]
        return remote(src(), dst, s_send.at[k, kind], s_recv.at[k, kind], device)

    def start(copy, s, *kinds):
        for kind in kinds:
            made = copy(s, kind)
            made.start()
            pending.append(made)

    def arrived(copy, s, *kinds):
        for kind in kinds:
            copy(s, kind).wait_recv()

    def own(s):
        start(gather_copy, s, 0, 3, 4, 1, 2)

    def mate(s):
        arrived(gather_copy, s, 4)
        start(gather_copy, s, 5, 6)

    def half_right(s):
        arrived(gather_copy, s, 0)
        start(gather_copy, s, 7)

    def half_left(s):
        arrived(gather_copy, s, 3)
        start(gather_copy, s, 8)

    def diagonal(s):
        arrived(gather_copy, s, 7)
        start(gather_copy, s, 9)
        arrived(gather_copy, s, 8)
        start(gather_copy, s, 10)

    def experts(s):
        i, e = s
        if s == (0, 0):
            loads[3].wait()
            loads[4].wait()
        arrived(gather_copy, s, 1, 2, 5, 6, 9, 10)
        block = gath[i, :, e]
        lhs = block.reshape(block.shape[0] * block.shape[1], block.shape[2])
        hidden = gelu(jnp.dot(lhs, w1[e], preferred_element_type=F32)).astype(BF16)
        result = jnp.dot(hidden, w2[e], preferred_element_type=F32)
        part[i, :, e] = result.astype(BF16).reshape(block.shape)
        start(scatter_copy, s, 0, 1, 2, 5, 6)

    def add(ref, *others):
        value = ref[...].astype(F32)
        for other in others:
            value = value + other.astype(F32)
        ref[...] = value.astype(BF16)

    def sum_diagonal(s):
        i, e = s
        arrived(scatter_copy, s, 0)
        add(part.at[i, at(2, False), e], r_l1[i * 2 + e])
        start(scatter_copy, s, 3, 4)

    def sum_mate(s):
        i, e = s
        arrived(scatter_copy, s, 1, 2)
        add(part.at[i, at(0, True), e], r_x[i * 2 + e, 0], r_x[i * 2 + e, 1])
        start(scatter_copy, s, 9)

    def sum_halves(s):
        i, e = s
        for k, dx in ((0, 1), (1, -1)):
            arrived(scatter_copy, s, 3 + k)
            add(part.at[i, at(dx, False), e, halves[k]], r_h[i * 2 + e, k])
            start(scatter_copy, s, 7 + k)

    def sum_own(s):
        i, e = s
        k = i * 2 + e
        arrived(scatter_copy, s, 5, 6, 7, 8, 9)
        value = part[i, n, e].astype(F32) + r_f[k, 0].astype(F32)
        value = value + r_f[k, 1].astype(F32) + r_l2[k].astype(F32)
        total[i, e] = value.astype(BF16)

    def give_back(i):
        both = total[i]
        both = both.reshape(2 * n_wide, both.shape[2])
        rows[...] = jnp.dot(order(True), both, preferred_element_type=F32)
        to_pairs(give2.at[i])
        to_all(give2.at[i], take2.at[i], 2 + i)

    def finish(i):
        from_all(give2.at[i], take2.at[i], 2 + i)
        from_pairs(take2.at[i])
        out_ref[i] = rows[...].astype(BF16)

    steps = (
        dispatch, unpack, own, mate, half_right, half_left, diagonal, experts,
        sum_diagonal, sum_mate, sum_halves, sum_own, give_back, finish,
    )
    steps = {step.__name__: step for step in steps}
    for name, what in plan:
        steps[name](what)

    for i in range(2):
        all_sent(give.at[i], i)
        all_sent(give2.at[i], 2 + i)
    for copy in pending:
        copy.wait_send()


def combine_kernel(comb_ref, out_ref, res_ref):
    res_ref[0] = lax.dot_general(
        comb_ref[0], out_ref[0], (((0,), (0,)), ((), ())), preferred_element_type=F32
    ).astype(BF16)


def per_device(n_wide, n_narrow, tokens, slot_params, expand_weight, reduce_weight):
    images, m, d = tokens.shape
    experts = slot_params.shape[0]
    block = (2, n_wide, d)
    vmem = pl.BlockSpec(memory_space=pltpu.VMEM)
    anyspace = pl.BlockSpec(memory_space=pl.ANY)
    dma = pltpu.SemaphoreType.DMA
    outs, comb = pl.pallas_call(
        functools.partial(exchange_kernel, n_wide, PLAN),
        out_shape=(
            jax.ShapeDtypeStruct((images, experts, d), BF16),
            jax.ShapeDtypeStruct((images, experts, m), BF16),
        ),
        in_specs=[anyspace] * 4,
        out_specs=(vmem, vmem),
        scratch_shapes=[
            pltpu.VMEM(tokens.shape, BF16),
            pltpu.VMEM(slot_params.shape, BF16),
            pltpu.VMEM(expand_weight.shape, BF16),
            pltpu.VMEM(reduce_weight.shape, BF16),
            pltpu.VMEM((experts, d), F32),
            pltpu.VMEM((2, n_wide, 2, d), BF16),
            pltpu.VMEM((2, n_wide, 2, d), BF16),
            pltpu.VMEM((2, n_narrow, *block), BF16),
            pltpu.VMEM((2, n_narrow, *block), BF16),
            pltpu.VMEM((4, n_wide, d), BF16),
            pltpu.VMEM((4, 2, n_wide, d), BF16),
            pltpu.VMEM((4, 2, n_wide // 2, d), BF16),
            pltpu.VMEM((4, 2, n_wide, d), BF16),
            pltpu.VMEM((4, n_wide, d), BF16),
            pltpu.VMEM((2, *block), BF16),
            pltpu.VMEM((2, n_wide, 2, d), BF16),
            pltpu.VMEM((2, n_wide, 2, d), BF16),
            dma((5,)), dma((4,)), dma((4,)), dma((4,)), dma((4, 11)), dma((4, 11)),
            dma((4, 10)), dma((4, 10)),
        ],
        compiler_params=pltpu.CompilerParams(
            collective_id=0, has_side_effects=True, vmem_limit_bytes=56 * 1024 * 1024
        ),
        name="exchange",
    )(tokens, slot_params, expand_weight, reduce_weight)
    return pl.pallas_call(
        combine_kernel,
        grid=(images,),
        out_shape=jax.ShapeDtypeStruct(tokens.shape, BF16),
        in_specs=[
            pl.BlockSpec((1, experts, m), lambda i: (i, 0, 0)),
            pl.BlockSpec((1, experts, d), lambda i: (i, 0, 0)),
        ],
        out_specs=pl.BlockSpec((1, m, d), lambda i: (i, 0, 0)),
        name="combine",
    )(comb, outs)


def solution(mesh):
    in_specs = (
        P(("wide", "narrow"), None, None),
        P(),
        P("wide", None, "narrow"),
        P("wide", "narrow", None),
    )
    return jax.shard_map(
        functools.partial(per_device, mesh.shape["wide"], mesh.shape["narrow"]),
        mesh=mesh,
        in_specs=in_specs,
        out_specs=P(("wide", "narrow"), None, None),
        check_vma=False,
    )
```

```python
import functools

import jax
import jax.numpy as jnp
from jax import lax
from jax.experimental import pallas as pl
from jax.experimental.pallas import tpu as pltpu
from jax.sharding import PartitionSpec as P

MESH = pl.DeviceIdType.MESH
NX = 4
NZ = 4
F32 = jnp.float32
BF16 = jnp.bfloat16

(
    DISPATCH, UNPACK, OWN, MATE, PASS, DIAGONAL, EXPERTS,
    SUM_DIAGONAL, SUM_MATE, SUM_HALF, SUM_OWN, GIVE_BACK, FINISH,
) = range(13)
PLAN = (
    (DISPATCH, 0), (DISPATCH, 1), (UNPACK, 0, 0), (OWN, (0, 0), 0), (OWN, (0, 1), 0), (UNPACK, 0, 1),
    (OWN, (0, 0), 1), (OWN, (0, 1), 1), (UNPACK, 1, 0), (OWN, (1, 1), 0), (OWN, (1, 0), 0), (PASS, (0, 0), 0),
    (MATE, (0, 0), 0), (PASS, (0, 1), 0), (MATE, (0, 1), 0), (UNPACK, 1, 1), (PASS, (0, 0), 1), (OWN, (1, 1), 1),
    (MATE, (0, 0), 1), (OWN, (1, 0), 1), (MATE, (0, 1), 1), (PASS, (0, 1), 1), (MATE, (1, 1), 0), (PASS, (1, 1), 0),
    (MATE, (1, 0), 0), (PASS, (1, 0), 0), (DIAGONAL, (0, 0), 0), (MATE, (1, 1), 1), (MATE, (1, 0), 1),
    (DIAGONAL, (0, 0), 1), (DIAGONAL, (0, 1), 0), (PASS, (1, 1), 1), (PASS, (1, 0), 1), (EXPERTS, (0, 0)),
    (DIAGONAL, (0, 1), 1), (DIAGONAL, (1, 1), 0), (DIAGONAL, (1, 0), 0), (SUM_DIAGONAL, (0, 0), 0),
    (DIAGONAL, (1, 1), 1), (SUM_DIAGONAL, (0, 0), 1), (DIAGONAL, (1, 0), 1), (EXPERTS, (0, 1)),
    (SUM_MATE, (0, 0), 1), (SUM_MATE, (0, 0), 0), (EXPERTS, (1, 1)), (EXPERTS, (1, 0)), (SUM_DIAGONAL, (0, 1), 1),
    (SUM_HALF, (0, 0), 1), (SUM_DIAGONAL, (0, 1), 0), (SUM_HALF, (0, 0), 0), (SUM_MATE, (0, 1), 1),
    (SUM_MATE, (0, 1), 0), (SUM_MATE, (1, 1), 0), (SUM_DIAGONAL, (1, 1), 0), (SUM_MATE, (1, 1), 1),
    (SUM_DIAGONAL, (1, 1), 1), (SUM_DIAGONAL, (1, 0), 0), (SUM_MATE, (1, 0), 0), (SUM_DIAGONAL, (1, 0), 1),
    (SUM_MATE, (1, 0), 1), (SUM_HALF, (0, 1), 0), (SUM_HALF, (0, 1), 1), (SUM_OWN, (0, 0), 0), (SUM_OWN, (0, 0), 1),
    (SUM_HALF, (1, 1), 0), (SUM_HALF, (1, 1), 1), (SUM_HALF, (1, 0), 0), (SUM_HALF, (1, 0), 1),
    (SUM_OWN, (0, 1), 0), (GIVE_BACK, 0, 0), (SUM_OWN, (0, 1), 1), (GIVE_BACK, 0, 1), (SUM_OWN, (1, 1), 0),
    (SUM_OWN, (1, 1), 1), (SUM_OWN, (1, 0), 0), (GIVE_BACK, 1, 0), (SUM_OWN, (1, 0), 1), (GIVE_BACK, 1, 1),
    (FINISH, 0), (FINISH, 1),
)


def gelu(v):
    return 0.5 * v * (1.0 + jnp.tanh(0.7978845608028654 * (v + 0.044715 * (v * v * v))))


def exchange_kernel(
    n_wide, plan,
    tok_hbm, slot_hbm, w1_hbm, w2_hbm,
    res_ref,
    tok, slot, w1, w2, rows, comb, give, take, gath, part, r_l1, r_x, r_h, r_f, r_l2, total, give2, take2,
    load_sem, own_sem, a_send, a_recv, g_send, g_recv, s_send, s_recv,
):
    w, n = lax.axis_index("wide"), lax.axis_index("narrow")
    x, z = n // 2, lax.rem(n, 2)
    group = n_wide // NZ
    w_group, w_place = w // group, lax.rem(w, group)
    half = n_wide // 2
    halves = (pl.ds(0, half), pl.ds(half, half))
    pending = []

    def at(dx, other):
        zz = 1 - z if other else z
        return lax.rem(x + dx + NX, NX) * 2 + zz

    right, left, mate_device = (w, at(1, False)), (w, at(-1, False)), (w, at(0, True))

    loads = [
        pltpu.make_async_copy(slot_hbm, slot, load_sem.at[0]),
        pltpu.make_async_copy(tok_hbm.at[0], tok.at[0], load_sem.at[1]),
        pltpu.make_async_copy(tok_hbm.at[1], tok.at[1], load_sem.at[2]),
        pltpu.make_async_copy(w1_hbm, w1, load_sem.at[3]),
        pltpu.make_async_copy(w2_hbm, w2, load_sem.at[4]),
    ]
    for load in loads[:3]:
        load.start()

    side = lax.rem(w_group + 3 - 2 * z, NZ)
    outward = (((2, x * 2 + 1 - z), (0, n)), ((1, x * 2), (3, x * 2 + 1)))
    homeward = (((2, x * 2 + 1 - z), (0, n)), ((None, x * 2), (None, x * 2 + 1)))

    barrier = pltpu.get_barrier_semaphore()

    def greet(to_group, to_narrow, first=0):
        @pl.loop(first, group)
        def _(q):
            to = to_group * group + lax.rem(w_place + q, group)
            pl.semaphore_signal(barrier, inc=1, device_id=(to, to_narrow), device_id_type=MESH)

    greet(w_group, n, 1)
    greet(lax.rem(w_group + 2, NZ), x * 2 + 1 - z)
    for k in range(2):
        greet(side, x * 2 + k)
    greet(lax.rem(w_group + 1 + 2 * z, NZ), n)
    for device in (right, left, mate_device):
        pl.semaphore_signal(barrier, inc=1, device_id=device, device_id_type=MESH)

    def remote(src, dst, send, recv, device):
        return pltpu.make_async_remote_copy(
            src_ref=src, dst_ref=dst, send_sem=send, recv_sem=recv,
            device_id=device, device_id_type=MESH,
        )

    def to_all(src, dst, k, h, by_owner):
        for j, (step, to_narrow) in enumerate((outward if by_owner else homeward)[h]):
            to_group = side if step is None else lax.rem(w_group + step, NZ)
            base = h * half + (j if not by_owner and h else z if h else 1 - j) * group

            @pl.loop(1 if step == 0 else 0, group)
            def _(q):
                place = lax.rem(w_place + q, group)
                to = to_group * group + place
                mine, theirs = (to, base + w_place) if by_owner else (base + place, w)
                remote(
                    src.at[mine], dst.at[theirs], a_send.at[k, h], a_recv.at[k, h], (to, to_narrow)
                ).start()

        if h == 0:
            own_copy(src, dst, k, by_owner).start()

    def own_copy(src, dst, k, by_owner):
        mine, theirs = (w, w_place) if by_owner else (w_place, w)
        return pltpu.make_async_copy(src.at[mine], dst.at[theirs], own_sem.at[k])

    def from_all(src, dst, k, h, by_owner):
        if h == 0:
            own_copy(src, dst, k, by_owner).wait()
        others = pl.ds(0, 2 * group - (h == 0))
        pltpu.make_async_copy(dst.at[others], dst.at[others], a_recv.at[k, h]).wait()

    def all_sent(src, k, h):
        others = pl.ds(0, 2 * group - (h == 0))
        pltpu.make_async_copy(src.at[others], src.at[others], a_send.at[k, h]).wait()

    def to_pairs(dst, first, count):
        for k in range(count):
            dst[first + k] = rows[2 * k : 2 * k + 2, :].astype(BF16)

    def from_pairs(src, first, count):
        for k in range(count):
            rows[2 * k : 2 * k + 2, :] = src[first + k].astype(F32)

    def order(count, back):
        shape = (2 * count, 2 * count)
        r, q = lax.broadcasted_iota(jnp.int32, shape, 0), lax.broadcasted_iota(jnp.int32, shape, 1)
        if back:
            r, q = q, r
        same = (r % count) * 2 + r // count == q
        return jnp.where(same, 1.0, 0.0).astype(BF16)

    def dispatch(i):
        for _ in range(1 if i else 2):
            loads.pop(0).wait()
        t = tok[i]
        logits = lax.dot_general(slot[...], t, (((1,), (1,)), ((), ())), preferred_element_type=F32)
        up = jnp.exp(logits - jnp.max(logits, axis=1, keepdims=True))
        weights = (up / jnp.sum(up, axis=1, keepdims=True)).astype(BF16)
        rows[...] = jnp.dot(weights, t, preferred_element_type=F32)
        to_pairs(give.at[i], 0, n_wide)
        if i == 0:
            pl.semaphore_wait(barrier, 5 * group - 1 + 3)
        for h in range(2):
            to_all(give.at[i], take.at[i], i, h, True)
        if i == 0:
            for load in loads[1:]:
                load.start()
        up = jnp.exp(logits - jnp.max(logits, axis=0, keepdims=True))
        comb[i] = (up / jnp.sum(up, axis=0, keepdims=True)).T.astype(BF16)

    def unpack(i, h):
        from_all(give.at[i], take.at[i], i, h, True)
        from_pairs(take.at[i], h * half, half)
        some = rows[0:n_wide, :].astype(BF16)
        by_expert = jnp.dot(order(half, False), some, preferred_element_type=F32)
        gath[i, n, :, halves[h], :] = by_expert.astype(BF16).reshape(2, half, by_expert.shape[1])

    def gather_copy(s, name):
        i, e = s
        kind, h = name
        g = gath.at[i]
        block, device, index = {
            "own right": (n, right, 0),
            "own left": (n, left, 2),
            "own mate": (n, mate_device, 4),
            "mate right": (at(0, True), right, 6),
            "mate left": (at(0, True), left, 8),
            "pass": (at(1 if h else -1, False), left if h else right, 10),
            "diagonal": (at(2, False), mate_device, 12),
        }[kind]
        ref = g.at[block, e, halves[h]]
        return remote(ref, ref, g_send.at[i * 2 + e, index + h], g_recv.at[i * 2 + e, index + h], device)

    def scatter_copy(s, name):
        i, e = s
        k = i * 2 + e
        kind, h = name
        block, dst, device, index = {
            "diagonal mate": (at(2, True), r_l1.at[k], mate_device, 0),
            "mate right": (at(1, True), r_x.at[k, 0], right, 2),
            "mate left": (at(-1, True), r_x.at[k, 1], left, 4),
            "pass": (at(2, False), r_h.at[k], left if h else right, 6),
            "own right": (at(1, False), r_f.at[k, 0], right, 8),
            "own left": (at(-1, False), r_f.at[k, 1], left, 10),
            "own mate": (at(0, True), r_l2.at[k], mate_device, 12),
        }[kind]
        return remote(
            part.at[i, block, e, halves[h]], dst.at[halves[h]],
            s_send.at[k, index + h], s_recv.at[k, index + h], device,
        )

    def start(copy, s, *names):
        for name in names:
            made = copy(s, name)
            made.start()
            pending.append(made)

    def arrived(copy, s, *names):
        for name in names:
            copy(s, name).wait_recv()

    def own(s, h):
        sides = ("own left", "own mate", "own right") if h else ("own right", "own mate", "own left")
        start(gather_copy, s, *((side, h) for side in sides))

    def mate(s, h):
        arrived(gather_copy, s, ("own mate", h))
        start(gather_copy, s, ("mate right", h), ("mate left", h))

    def pass_on(s, h):
        arrived(gather_copy, s, ("own left" if h else "own right", h))
        start(gather_copy, s, ("pass", h))

    def diagonal(s, h):
        arrived(gather_copy, s, ("pass", h))
        start(gather_copy, s, ("diagonal", h))

    def experts(s):
        i, e = s
        while loads:
            loads.pop().wait()
        arrived(gather_copy, s, ("own right", 1), ("own left", 0))
        for h in range(2):
            arrived(gather_copy, s, ("mate right", h), ("mate left", h), ("diagonal", h))
        block = gath[i, :, e]
        lhs = block.reshape(block.shape[0] * block.shape[1], block.shape[2])
        hidden = gelu(jnp.dot(lhs, w1[e], preferred_element_type=F32)).astype(BF16)
        result = jnp.dot(hidden, w2[e], preferred_element_type=F32)
        part[i, :, e] = result.astype(BF16).reshape(block.shape)
        for h in range(2):
            start(scatter_copy, s, ("diagonal mate", h), ("mate right", h), ("mate left", h))
        start(scatter_copy, s, ("own right", 1), ("own left", 0))

    def add(ref, *others):
        value = ref[...].astype(F32)
        for other in others:
            value = value + other.astype(F32)
        ref[...] = value.astype(BF16)

    def sum_diagonal(s, h):
        i, e = s
        arrived(scatter_copy, s, ("diagonal mate", h))
        add(part.at[i, at(2, False), e, halves[h]], r_l1[i * 2 + e, halves[h]])
        start(scatter_copy, s, ("pass", h))

    def sum_mate(s, h):
        i, e = s
        k = i * 2 + e
        arrived(scatter_copy, s, ("mate right", h), ("mate left", h))
        add(part.at[i, at(0, True), e, halves[h]], r_x[k, 0, halves[h]], r_x[k, 1, halves[h]])
        start(scatter_copy, s, ("own mate", h))

    def sum_half(s, h):
        i, e = s
        arrived(scatter_copy, s, ("pass", h))
        add(part.at[i, at(-1 if h else 1, False), e, halves[h]], r_h[i * 2 + e, halves[h]])
        start(scatter_copy, s, ("own left" if h else "own right", h))

    def sum_own(s, h):
        i, e = s
        k = i * 2 + e
        arrived(scatter_copy, s, ("own right", h), ("own left", h), ("own mate", h))
        value = part[i, n, e, halves[h]].astype(F32) + r_f[k, 0, halves[h]].astype(F32)
        value = value + r_f[k, 1, halves[h]].astype(F32) + r_l2[k, halves[h]].astype(F32)
        total[i, h, e] = value.astype(BF16)

    def give_back(i, h):
        both = total[i, h]
        both = both.reshape(2 * half, both.shape[2])
        rows[0:n_wide, :] = jnp.dot(order(half, True), both, preferred_element_type=F32)
        to_pairs(give2.at[i], h * half, half)
        to_all(give2.at[i], take2.at[i], 2 + i, h, False)

    def finish(i):
        for h in range(2):
            from_all(give2.at[i], take2.at[i], 2 + i, h, False)
        from_pairs(take2.at[i], 0, n_wide)
        res_ref[i] = jnp.dot(comb[i], rows[...].astype(BF16), preferred_element_type=F32).astype(BF16)

    steps = (
        dispatch, unpack, own, mate, pass_on, diagonal, experts,
        sum_diagonal, sum_mate, sum_half, sum_own, give_back, finish,
    )
    for name, *what in plan:
        steps[name](*what)

    for h in range(2):
        for i in range(2):
            all_sent(give.at[i], i, h)
            all_sent(give2.at[i], 2 + i, h)
    for copy in pending:
        copy.wait_send()


def per_device(n_wide, n_narrow, tokens, slot_params, expand_weight, reduce_weight):
    images, m, d = tokens.shape
    experts = slot_params.shape[0]
    rows = (n_wide, d)
    anyspace = pl.BlockSpec(memory_space=pl.ANY)
    dma = pltpu.SemaphoreType.DMA
    return pl.pallas_call(
        functools.partial(exchange_kernel, n_wide, PLAN),
        out_shape=pltpu.VMEM(tokens.shape, BF16),
        in_specs=[anyspace] * 4,
        out_specs=pl.BlockSpec(memory_space=pltpu.VMEM),
        scratch_shapes=[
            pltpu.VMEM(tokens.shape, BF16),
            pltpu.VMEM(slot_params.shape, BF16),
            pltpu.VMEM(expand_weight.shape, BF16),
            pltpu.VMEM(reduce_weight.shape, BF16),
            pltpu.VMEM((experts, d), F32),
            pltpu.VMEM((images, m, experts), BF16),
            pltpu.VMEM((2, n_wide, 2, d), BF16),
            pltpu.VMEM((2, n_wide, 2, d), BF16),
            pltpu.VMEM((2, n_narrow, 2, *rows), BF16),
            pltpu.VMEM((2, n_narrow, 2, *rows), BF16),
            pltpu.VMEM((4, *rows), BF16),
            pltpu.VMEM((4, 2, *rows), BF16),
            pltpu.VMEM((4, *rows), BF16),
            pltpu.VMEM((4, 2, *rows), BF16),
            pltpu.VMEM((4, *rows), BF16),
            pltpu.VMEM((2, 2, 2, n_wide // 2, d), BF16),
            pltpu.VMEM((2, n_wide, 2, d), BF16),
            pltpu.VMEM((2, n_wide, 2, d), BF16),
            dma((5,)), dma((4,)), dma((4, 2)), dma((4, 2)), dma((4, 14)), dma((4, 14)),
            dma((4, 14)), dma((4, 14)),
        ],
        compiler_params=pltpu.CompilerParams(
            collective_id=0, has_side_effects=True, vmem_limit_bytes=56 * 1024 * 1024
        ),
        name="exchange",
    )(tokens, slot_params, expand_weight, reduce_weight)


def solution(mesh):
    in_specs = (
        P(("wide", "narrow"), None, None),
        P(),
        P("wide", None, "narrow"),
        P("wide", "narrow", None),
    )
    return jax.shard_map(
        functools.partial(per_device, mesh.shape["wide"], mesh.shape["narrow"]),
        mesh=mesh,
        in_specs=in_specs,
        out_specs=P(("wide", "narrow"), None, None),
        check_vma=False,
    )
```

```python
import functools

import jax
import jax.numpy as jnp
from jax import lax
from jax.experimental import pallas as pl
from jax.experimental.pallas import tpu as pltpu
from jax.sharding import PartitionSpec as P

MESH = pl.DeviceIdType.MESH
NX = 4
NZ = 4
F32 = jnp.float32
BF16 = jnp.bfloat16

(
    DISPATCH, UNPACK, OWN, MATE, PASS, DIAGONAL, EXPERTS,
    SUM_DIAGONAL, SUM_MATE, SUM_HALF, SUM_OWN, GIVE_BACK, FINISH,
) = range(13)
PLAN = (
    (DISPATCH, 0), (DISPATCH, 1), (UNPACK, 0, 0), (OWN, (0, 0), 0), (OWN, (0, 1), 0), (UNPACK, 0, 1),
    (OWN, (0, 0), 1), (OWN, (0, 1), 1), (UNPACK, 1, 0), (MATE, (0, 0), 0), (PASS, (0, 0), 0), (OWN, (1, 1), 0),
    (OWN, (1, 0), 0), (PASS, (0, 1), 0), (MATE, (0, 1), 0), (UNPACK, 1, 1), (PASS, (0, 0), 1), (MATE, (0, 0), 1),
    (OWN, (1, 0), 1), (OWN, (1, 1), 1), (MATE, (0, 1), 1), (PASS, (0, 1), 1), (MATE, (1, 1), 0),
    (DIAGONAL, (0, 0), 0), (MATE, (1, 0), 0), (PASS, (1, 1), 0), (MATE, (1, 0), 1), (PASS, (1, 0), 0),
    (MATE, (1, 1), 1), (DIAGONAL, (0, 0), 1), (DIAGONAL, (0, 1), 0), (PASS, (1, 0), 1), (PASS, (1, 1), 1),
    (EXPERTS, (0, 0)), (DIAGONAL, (0, 1), 1), (DIAGONAL, (1, 1), 0), (SUM_DIAGONAL, (0, 0), 0),
    (DIAGONAL, (1, 0), 1), (DIAGONAL, (1, 0), 0), (SUM_DIAGONAL, (0, 0), 1), (DIAGONAL, (1, 1), 1),
    (EXPERTS, (0, 1)), (SUM_MATE, (0, 0), 1), (SUM_MATE, (0, 0), 0), (EXPERTS, (1, 0)), (SUM_HALF, (0, 0), 1),
    (SUM_HALF, (0, 0), 0), (SUM_DIAGONAL, (0, 1), 0), (EXPERTS, (1, 1)), (SUM_DIAGONAL, (0, 1), 1),
    (SUM_MATE, (0, 1), 1), (SUM_MATE, (0, 1), 0), (SUM_MATE, (1, 0), 0), (SUM_DIAGONAL, (1, 0), 0),
    (SUM_MATE, (1, 0), 1), (SUM_DIAGONAL, (1, 0), 1), (SUM_DIAGONAL, (1, 1), 0), (SUM_OWN, (0, 0), 0),
    (SUM_OWN, (0, 0), 1), (SUM_DIAGONAL, (1, 1), 1), (SUM_HALF, (0, 1), 0), (SUM_MATE, (1, 1), 0),
    (SUM_MATE, (1, 1), 1), (SUM_HALF, (0, 1), 1), (SUM_HALF, (1, 0), 0), (SUM_HALF, (1, 0), 1),
    (SUM_HALF, (1, 1), 0), (SUM_HALF, (1, 1), 1), (SUM_OWN, (0, 1), 0), (GIVE_BACK, 0, 0), (SUM_OWN, (0, 1), 1),
    (GIVE_BACK, 0, 1), (SUM_OWN, (1, 0), 0), (SUM_OWN, (1, 0), 1), (SUM_OWN, (1, 1), 0), (GIVE_BACK, 1, 0),
    (SUM_OWN, (1, 1), 1), (GIVE_BACK, 1, 1), (FINISH, 0), (FINISH, 1),
)


def gelu(v):
    return 0.5 * v * (1.0 + jnp.tanh(0.7978845608028654 * (v + 0.044715 * (v * v * v))))


def exchange_kernel(
    n_wide, plan,
    tok_hbm, slot_hbm, w1_hbm, w2_hbm,
    res_ref,
    tok, slot, w1, w2, rows, comb, give, take, gath, part, r_l1, r_x, r_h, r_f, r_l2, total, give2, take2,
    load_sem, own_sem, a_send, a_recv, g_send, g_recv, s_send, s_recv,
):
    w, n = lax.axis_index("wide"), lax.axis_index("narrow")
    x, z = n // 2, lax.rem(n, 2)
    group = n_wide // NZ
    w_group, w_place = w // group, lax.rem(w, group)
    half = n_wide // 2
    halves = (pl.ds(0, half), pl.ds(half, half))
    pending = []

    def at(dx, other):
        zz = 1 - z if other else z
        return lax.rem(x + dx + NX, NX) * 2 + zz

    right, left, mate_device = (w, at(1, False)), (w, at(-1, False)), (w, at(0, True))

    loads = [
        pltpu.make_async_copy(slot_hbm, slot, load_sem.at[0]),
        pltpu.make_async_copy(tok_hbm.at[0], tok.at[0], load_sem.at[1]),
        pltpu.make_async_copy(tok_hbm.at[1], tok.at[1], load_sem.at[2]),
        pltpu.make_async_copy(w1_hbm, w1, load_sem.at[3]),
        pltpu.make_async_copy(w2_hbm, w2, load_sem.at[4]),
    ]
    for load in loads[:3]:
        load.start()

    other = x * 2 + 1 - z
    near, away = 3 - 2 * z, 1 + 2 * z
    outward = (((0, n), (near, other)), ((away, n), (2, other)))
    homeward = (((0, n), (near, other)), ((near, n), (2, other)))

    barrier = pltpu.get_barrier_semaphore()

    for first, step, to_narrow in ((0, 2, other), (0, away, n), (0, near, n), (0, near, other), (1, 0, n)):
        to_group = lax.rem(w_group + step, NZ) * group

        @pl.loop(first, group)
        def _(q):
            to = to_group + lax.rem(w_place + q, group)
            pl.semaphore_signal(barrier, inc=1, device_id=(to, to_narrow), device_id_type=MESH)

    for device in (right, left, mate_device):
        pl.semaphore_signal(barrier, inc=1, device_id=device, device_id_type=MESH)

    def remote(src, dst, send, recv, device):
        return pltpu.make_async_remote_copy(
            src_ref=src, dst_ref=dst, send_sem=send, recv_sem=recv,
            device_id=device, device_id_type=MESH,
        )

    def to_all(src, dst, k, h, by_owner):
        for j in (1, 0):
            step, to_narrow = (outward if by_owner else homeward)[h][j]
            to_group = lax.rem(w_group + step, NZ) * group
            base = h * half + j * group

            @pl.loop(0 if h or j else 1, group)
            def _(q):
                place = lax.rem(w_place + q, group)
                to = to_group + place
                mine, theirs = (to, base + w_place) if by_owner else (base + place, w)
                remote(
                    src.at[mine], dst.at[theirs], a_send.at[k, h], a_recv.at[k, h], (to, to_narrow)
                ).start()

        if h == 0:
            own_copy(src, dst, k, by_owner).start()

    def own_copy(src, dst, k, by_owner):
        mine, theirs = (w, w_place) if by_owner else (w_place, w)
        return pltpu.make_async_copy(src.at[mine], dst.at[theirs], own_sem.at[k])

    def from_all(src, dst, k, h, by_owner):
        if h == 0:
            own_copy(src, dst, k, by_owner).wait()
        others = pl.ds(0, 2 * group - (h == 0))
        pltpu.make_async_copy(dst.at[others], dst.at[others], a_recv.at[k, h]).wait()

    def all_sent(src, k, h):
        others = pl.ds(0, 2 * group - (h == 0))
        pltpu.make_async_copy(src.at[others], src.at[others], a_send.at[k, h]).wait()

    def to_pairs(dst, first, count):
        for k in range(count):
            dst[first + k] = rows[2 * k : 2 * k + 2, :].astype(BF16)

    def from_pairs(src, first, count):
        for k in range(count):
            rows[2 * k : 2 * k + 2, :] = src[first + k].astype(F32)

    def order(count, back):
        shape = (2 * count, 2 * count)
        r, q = lax.broadcasted_iota(jnp.int32, shape, 0), lax.broadcasted_iota(jnp.int32, shape, 1)
        if back:
            r, q = q, r
        same = (r % count) * 2 + r // count == q
        return jnp.where(same, 1.0, 0.0).astype(BF16)

    def dispatch(i):
        for _ in range(1 if i else 2):
            loads.pop(0).wait()
        t = tok[i]
        logits = lax.dot_general(slot[...], t, (((1,), (1,)), ((), ())), preferred_element_type=F32)
        up = jnp.exp(logits - jnp.max(logits, axis=1, keepdims=True))
        weights = (up / jnp.sum(up, axis=1, keepdims=True)).astype(BF16)
        rows[...] = jnp.dot(weights, t, preferred_element_type=F32)
        to_pairs(give.at[i], 0, n_wide)
        if i == 0:
            pl.semaphore_wait(barrier, 5 * group - 1 + 3)
        for h in range(2):
            to_all(give.at[i], take.at[i], i, h, True)
        if i == 0:
            for load in loads[1:]:
                load.start()
        up = jnp.exp(logits - jnp.max(logits, axis=0, keepdims=True))
        comb[i] = (up / jnp.sum(up, axis=0, keepdims=True)).T.astype(BF16)

    def unpack(i, h):
        from_all(give.at[i], take.at[i], i, h, True)
        from_pairs(take.at[i], h * half, half)
        some = rows[0:n_wide, :].astype(BF16)
        by_expert = jnp.dot(order(half, False), some, preferred_element_type=F32)
        gath[i, n, :, halves[h], :] = by_expert.astype(BF16).reshape(2, half, by_expert.shape[1])

    def gather_copy(s, name):
        i, e = s
        kind, h = name
        g = gath.at[i]
        block, device, index = {
            "own right": (n, right, 0),
            "own left": (n, left, 2),
            "own mate": (n, mate_device, 4),
            "mate right": (at(0, True), right, 6),
            "mate left": (at(0, True), left, 8),
            "pass": (at(1 if h else -1, False), left if h else right, 10),
            "diagonal": (at(2, False), mate_device, 12),
        }[kind]
        ref = g.at[block, e, halves[h]]
        return remote(ref, ref, g_send.at[i * 2 + e, index + h], g_recv.at[i * 2 + e, index + h], device)

    def scatter_copy(s, name):
        i, e = s
        k = i * 2 + e
        kind, h = name
        block, dst, device, index = {
            "diagonal mate": (at(2, True), r_l1.at[k], mate_device, 0),
            "mate right": (at(1, True), r_x.at[k, 0], right, 2),
            "mate left": (at(-1, True), r_x.at[k, 1], left, 4),
            "pass": (at(2, False), r_h.at[k], left if h else right, 6),
            "own right": (at(1, False), r_f.at[k, 0], right, 8),
            "own left": (at(-1, False), r_f.at[k, 1], left, 10),
            "own mate": (at(0, True), r_l2.at[k], mate_device, 12),
        }[kind]
        return remote(
            part.at[i, block, e, halves[h]], dst.at[halves[h]],
            s_send.at[k, index + h], s_recv.at[k, index + h], device,
        )

    def start(copy, s, *names):
        for name in names:
            made = copy(s, name)
            made.start()
            pending.append(made)

    def arrived(copy, s, *names):
        for name in names:
            copy(s, name).wait_recv()

    def own(s, h):
        sides = ("own left", "own mate", "own right") if h else ("own right", "own mate", "own left")
        start(gather_copy, s, *((side, h) for side in sides))

    def mate(s, h):
        arrived(gather_copy, s, ("own mate", h))
        start(gather_copy, s, ("mate right", h), ("mate left", h))

    def pass_on(s, h):
        arrived(gather_copy, s, ("own left" if h else "own right", h))
        start(gather_copy, s, ("pass", h))

    def diagonal(s, h):
        arrived(gather_copy, s, ("pass", h))
        start(gather_copy, s, ("diagonal", h))

    def experts(s):
        i, e = s
        while loads:
            loads.pop().wait()
        arrived(gather_copy, s, ("own right", 1), ("own left", 0))
        for h in range(2):
            arrived(gather_copy, s, ("mate right", h), ("mate left", h), ("diagonal", h))
        block = gath[i, :, e]
        lhs = block.reshape(block.shape[0] * block.shape[1], block.shape[2])
        hidden = gelu(jnp.dot(lhs, w1[e], preferred_element_type=F32)).astype(BF16)
        result = jnp.dot(hidden, w2[e], preferred_element_type=F32)
        part[i, :, e] = result.astype(BF16).reshape(block.shape)
        for h in range(2):
            start(scatter_copy, s, ("diagonal mate", h), ("mate right", h), ("mate left", h))
        start(scatter_copy, s, ("own right", 1), ("own left", 0))

    def add(ref, *others):
        value = ref[...].astype(F32)
        for other in others:
            value = value + other.astype(F32)
        ref[...] = value.astype(BF16)

    def sum_diagonal(s, h):
        i, e = s
        arrived(scatter_copy, s, ("diagonal mate", h))
        add(part.at[i, at(2, False), e, halves[h]], r_l1[i * 2 + e, halves[h]])
        start(scatter_copy, s, ("pass", h))

    def sum_mate(s, h):
        i, e = s
        k = i * 2 + e
        arrived(scatter_copy, s, ("mate right", h), ("mate left", h))
        add(part.at[i, at(0, True), e, halves[h]], r_x[k, 0, halves[h]], r_x[k, 1, halves[h]])
        start(scatter_copy, s, ("own mate", h))

    def sum_half(s, h):
        i, e = s
        arrived(scatter_copy, s, ("pass", h))
        add(part.at[i, at(-1 if h else 1, False), e, halves[h]], r_h[i * 2 + e, halves[h]])
        start(scatter_copy, s, ("own left" if h else "own right", h))

    def sum_own(s, h):
        i, e = s
        k = i * 2 + e
        arrived(scatter_copy, s, ("own right", h), ("own left", h), ("own mate", h))
        value = part[i, n, e, halves[h]].astype(F32) + r_f[k, 0, halves[h]].astype(F32)
        value = value + r_f[k, 1, halves[h]].astype(F32) + r_l2[k, halves[h]].astype(F32)
        total[i, h, e] = value.astype(BF16)

    def give_back(i, h):
        both = total[i, h]
        both = both.reshape(2 * half, both.shape[2])
        rows[0:n_wide, :] = jnp.dot(order(half, True), both, preferred_element_type=F32)
        to_pairs(give2.at[i], h * half, half)
        to_all(give2.at[i], take2.at[i], 2 + i, h, False)

    def finish(i):
        for h in range(2):
            from_all(give2.at[i], take2.at[i], 2 + i, h, False)
        from_pairs(take2.at[i], 0, n_wide)
        res_ref[i] = jnp.dot(comb[i], rows[...].astype(BF16), preferred_element_type=F32).astype(BF16)

    steps = (
        dispatch, unpack, own, mate, pass_on, diagonal, experts,
        sum_diagonal, sum_mate, sum_half, sum_own, give_back, finish,
    )
    for name, *what in plan:
        steps[name](*what)

    for h in range(2):
        for i in range(2):
            all_sent(give.at[i], i, h)
            all_sent(give2.at[i], 2 + i, h)
    for copy in pending:
        copy.wait_send()


def per_device(n_wide, n_narrow, tokens, slot_params, expand_weight, reduce_weight):
    images, m, d = tokens.shape
    experts = slot_params.shape[0]
    rows = (n_wide, d)
    anyspace = pl.BlockSpec(memory_space=pl.ANY)
    dma = pltpu.SemaphoreType.DMA
    return pl.pallas_call(
        functools.partial(exchange_kernel, n_wide, PLAN),
        out_shape=pltpu.VMEM(tokens.shape, BF16),
        in_specs=[anyspace] * 4,
        out_specs=pl.BlockSpec(memory_space=pltpu.VMEM),
        scratch_shapes=[
            pltpu.VMEM(tokens.shape, BF16),
            pltpu.VMEM(slot_params.shape, BF16),
            pltpu.VMEM(expand_weight.shape, BF16),
            pltpu.VMEM(reduce_weight.shape, BF16),
            pltpu.VMEM((experts, d), F32),
            pltpu.VMEM((images, m, experts), BF16),
            pltpu.VMEM((2, n_wide, 2, d), BF16),
            pltpu.VMEM((2, n_wide, 2, d), BF16),
            pltpu.VMEM((2, n_narrow, 2, *rows), BF16),
            pltpu.VMEM((2, n_narrow, 2, *rows), BF16),
            pltpu.VMEM((4, *rows), BF16),
            pltpu.VMEM((4, 2, *rows), BF16),
            pltpu.VMEM((4, *rows), BF16),
            pltpu.VMEM((4, 2, *rows), BF16),
            pltpu.VMEM((4, *rows), BF16),
            pltpu.VMEM((2, 2, 2, n_wide // 2, d), BF16),
            pltpu.VMEM((2, n_wide, 2, d), BF16),
            pltpu.VMEM((2, n_wide, 2, d), BF16),
            dma((5,)), dma((4,)), dma((4, 2)), dma((4, 2)), dma((4, 14)), dma((4, 14)),
            dma((4, 14)), dma((4, 14)),
        ],
        compiler_params=pltpu.CompilerParams(
            collective_id=0, has_side_effects=True, vmem_limit_bytes=56 * 1024 * 1024
        ),
        name="exchange",
    )(tokens, slot_params, expand_weight, reduce_weight)


def solution(mesh):
    in_specs = (
        P(("wide", "narrow"), None, None),
        P(),
        P("wide", None, "narrow"),
        P("wide", "narrow", None),
    )
    return jax.shard_map(
        functools.partial(per_device, mesh.shape["wide"], mesh.shape["narrow"]),
        mesh=mesh,
        in_specs=in_specs,
        out_specs=P(("wide", "narrow"), None, None),
        check_vma=False,
    )
```

```python
import functools

import jax
import jax.numpy as jnp
from jax import lax
from jax.experimental import pallas as pl
from jax.experimental.pallas import tpu as pltpu
from jax.sharding import PartitionSpec as P

MESH = pl.DeviceIdType.MESH
NX = 4
NZ = 4
F32 = jnp.float32
BF16 = jnp.bfloat16

(
    DISPATCH, UNPACK, OWN, MATE, PASS, DIAGONAL, EXPERTS,
    SUM_DIAGONAL, SUM_MATE, SUM_HALF, SUM_OWN, GIVE_BACK, FINISH,
) = range(13)
PLAN = (
    (DISPATCH, 0), (DISPATCH, 1), (UNPACK, 0, 0), (OWN, (0, 0), 0), (OWN, (0, 1), 0), (UNPACK, 0, 1),
    (OWN, (0, 0), 1), (OWN, (0, 1), 1), (UNPACK, 1, 0), (MATE, (0, 0), 0), (PASS, (0, 0), 0), (OWN, (1, 1), 0),
    (OWN, (1, 0), 0), (PASS, (0, 1), 0), (MATE, (0, 1), 0), (UNPACK, 1, 1), (PASS, (0, 0), 1), (MATE, (0, 0), 1),
    (OWN, (1, 0), 1), (OWN, (1, 1), 1), (MATE, (0, 1), 1), (PASS, (0, 1), 1), (MATE, (1, 1), 0),
    (DIAGONAL, (0, 0), 0), (MATE, (1, 0), 0), (PASS, (1, 1), 0), (MATE, (1, 0), 1), (PASS, (1, 0), 0),
    (MATE, (1, 1), 1), (DIAGONAL, (0, 0), 1), (DIAGONAL, (0, 1), 0), (PASS, (1, 0), 1), (PASS, (1, 1), 1),
    (EXPERTS, (0, 0)), (DIAGONAL, (0, 1), 1), (DIAGONAL, (1, 1), 0), (SUM_DIAGONAL, (0, 0), 0),
    (DIAGONAL, (1, 0), 1), (DIAGONAL, (1, 0), 0), (SUM_DIAGONAL, (0, 0), 1), (DIAGONAL, (1, 1), 1),
    (EXPERTS, (0, 1)), (SUM_MATE, (0, 0), 1), (SUM_MATE, (0, 0), 0), (EXPERTS, (1, 0)), (SUM_HALF, (0, 0), 1),
    (SUM_HALF, (0, 0), 0), (SUM_DIAGONAL, (0, 1), 0), (EXPERTS, (1, 1)), (SUM_DIAGONAL, (0, 1), 1),
    (SUM_MATE, (0, 1), 1), (SUM_MATE, (0, 1), 0), (SUM_MATE, (1, 0), 1), (SUM_DIAGONAL, (1, 0), 1),
    (SUM_MATE, (1, 0), 0), (SUM_DIAGONAL, (1, 0), 0), (SUM_DIAGONAL, (1, 1), 1), (SUM_OWN, (0, 0), 0),
    (SUM_OWN, (0, 0), 1), (SUM_DIAGONAL, (1, 1), 0), (SUM_HALF, (0, 1), 0), (SUM_MATE, (1, 1), 1),
    (SUM_MATE, (1, 1), 0), (SUM_HALF, (0, 1), 1), (SUM_HALF, (1, 0), 1), (SUM_HALF, (1, 1), 1),
    (SUM_HALF, (1, 0), 0), (SUM_HALF, (1, 1), 0), (SUM_OWN, (0, 1), 0), (GIVE_BACK, 0, 0), (SUM_OWN, (0, 1), 1),
    (GIVE_BACK, 0, 1), (SUM_OWN, (1, 0), 1), (SUM_OWN, (1, 1), 1), (GIVE_BACK, 1, 1), (SUM_OWN, (1, 0), 0),
    (SUM_OWN, (1, 1), 0), (GIVE_BACK, 1, 0), (FINISH, 0), (FINISH, 1),
)


def gelu(v):
    return 0.5 * v * (1.0 + jnp.tanh(0.7978845608028654 * (v + 0.044715 * (v * v * v))))


def exchange_kernel(
    n_wide, plan,
    tok_hbm, slot_hbm, w1_hbm, w2_hbm,
    res_ref,
    tok, slot, w1, w2, rows, comb, give, take, gath, part, r_l1, r_x, r_h, r_f, r_l2, total, give2, take2,
    load_sem, own_sem, a_send, a_recv, g_send, g_recv, s_send, s_recv,
):
    w, n = lax.axis_index("wide"), lax.axis_index("narrow")
    x, z = n // 2, lax.rem(n, 2)
    group = n_wide // NZ
    w_group, w_place = w // group, lax.rem(w, group)
    half = n_wide // 2
    halves = (pl.ds(0, half), pl.ds(half, half))
    pending = []

    def at(dx, other):
        zz = 1 - z if other else z
        return lax.rem(x + dx + NX, NX) * 2 + zz

    right, left, mate_device = (w, at(1, False)), (w, at(-1, False)), (w, at(0, True))

    quarter = tok.shape[1] // 4
    loads = [pltpu.make_async_copy(slot_hbm, slot, load_sem.at[0])]
    for k in range(4):
        rows_k = pl.ds(k * quarter, quarter)
        loads.append(pltpu.make_async_copy(tok_hbm.at[0, rows_k], tok.at[0, rows_k], load_sem.at[1 + k]))
    loads += [
        pltpu.make_async_copy(tok_hbm.at[1], tok.at[1], load_sem.at[5]),
        pltpu.make_async_copy(w1_hbm, w1, load_sem.at[6]),
        pltpu.make_async_copy(w2_hbm, w2, load_sem.at[7]),
    ]
    for load in loads[:6]:
        load.start()

    other = x * 2 + 1 - z
    near, away = 3 - 2 * z, 1 + 2 * z
    outward = (((0, n), (near, other)), ((away, n), (2, other)))
    homeward = (((0, n), (near, other)), ((near, n), (2, other)))

    barrier = pltpu.get_barrier_semaphore()

    for first, step, to_narrow in ((0, 2, other), (0, away, n), (0, near, n), (0, near, other), (1, 0, n)):
        to_group = lax.rem(w_group + step, NZ) * group

        @pl.loop(first, group)
        def _(q):
            to = to_group + lax.rem(w_place + q, group)
            pl.semaphore_signal(barrier, inc=1, device_id=(to, to_narrow), device_id_type=MESH)

    for device in (right, left, mate_device):
        pl.semaphore_signal(barrier, inc=1, device_id=device, device_id_type=MESH)

    def remote(src, dst, send, recv, device):
        return pltpu.make_async_remote_copy(
            src_ref=src, dst_ref=dst, send_sem=send, recv_sem=recv,
            device_id=device, device_id_type=MESH,
        )

    def to_all(src, dst, k, h, by_owner):
        for j in (1, 0):
            step, to_narrow = (outward if by_owner else homeward)[h][j]
            to_group = lax.rem(w_group + step, NZ) * group
            base = h * half + j * group

            @pl.loop(0 if h or j else 1, group)
            def _(q):
                place = lax.rem(w_place + q, group)
                to = to_group + place
                mine, theirs = (to, base + w_place) if by_owner else (base + place, w)
                remote(
                    src.at[mine], dst.at[theirs], a_send.at[k, h], a_recv.at[k, h], (to, to_narrow)
                ).start()

        if h == 0:
            own_copy(src, dst, k, by_owner).start()

    def own_copy(src, dst, k, by_owner):
        mine, theirs = (w, w_place) if by_owner else (w_place, w)
        return pltpu.make_async_copy(src.at[mine], dst.at[theirs], own_sem.at[k])

    def from_all(src, dst, k, h, by_owner):
        if h == 0:
            own_copy(src, dst, k, by_owner).wait()
        others = pl.ds(0, 2 * group - (h == 0))
        pltpu.make_async_copy(dst.at[others], dst.at[others], a_recv.at[k, h]).wait()

    def all_sent(src, k, h):
        others = pl.ds(0, 2 * group - (h == 0))
        pltpu.make_async_copy(src.at[others], src.at[others], a_send.at[k, h]).wait()

    def to_pairs(dst, first, count):
        for k in range(count):
            dst[first + k] = rows[2 * k : 2 * k + 2, :].astype(BF16)

    def from_pairs(src, first, count):
        for k in range(count):
            rows[2 * k : 2 * k + 2, :] = src[first + k].astype(F32)

    def order(count, back):
        shape = (2 * count, 2 * count)
        r, q = lax.broadcasted_iota(jnp.int32, shape, 0), lax.broadcasted_iota(jnp.int32, shape, 1)
        if back:
            r, q = q, r
        same = (r % count) * 2 + r // count == q
        return jnp.where(same, 1.0, 0.0).astype(BF16)

    def dispatch(i):
        for _ in range(1 if i else 5):
            loads.pop(0).wait()
        t = tok[i]
        logits = lax.dot_general(slot[...], t, (((1,), (1,)), ((), ())), preferred_element_type=F32)
        up = jnp.exp(logits - jnp.max(logits, axis=1, keepdims=True))
        weights = (up / jnp.sum(up, axis=1, keepdims=True)).astype(BF16)
        rows[...] = jnp.dot(weights, t, preferred_element_type=F32)
        to_pairs(give.at[i], 0, n_wide)
        if i == 0:
            pl.semaphore_wait(barrier, 5 * group - 1 + 3)
        for h in range(2):
            to_all(give.at[i], take.at[i], i, h, True)
        if i == 0:
            for load in loads[1:]:
                load.start()
        up = jnp.exp(logits - jnp.max(logits, axis=0, keepdims=True))
        comb[i] = (up / jnp.sum(up, axis=0, keepdims=True)).T.astype(BF16)

    def unpack(i, h):
        from_all(give.at[i], take.at[i], i, h, True)
        from_pairs(take.at[i], h * half, half)
        some = rows[0:n_wide, :].astype(BF16)
        by_expert = jnp.dot(order(half, False), some, preferred_element_type=F32)
        gath[i, n, :, halves[h], :] = by_expert.astype(BF16).reshape(2, half, by_expert.shape[1])

    def gather_copy(s, name):
        i, e = s
        kind, h = name
        g = gath.at[i]
        block, device, index = {
            "own right": (n, right, 0),
            "own left": (n, left, 2),
            "own mate": (n, mate_device, 4),
            "mate right": (at(0, True), right, 6),
            "mate left": (at(0, True), left, 8),
            "pass": (at(1 if h else -1, False), left if h else right, 10),
            "diagonal": (at(2, False), mate_device, 12),
        }[kind]
        ref = g.at[block, e, halves[h]]
        return remote(ref, ref, g_send.at[i * 2 + e, index + h], g_recv.at[i * 2 + e, index + h], device)

    def scatter_copy(s, name):
        i, e = s
        k = i * 2 + e
        kind, h = name
        block, dst, device, index = {
            "diagonal mate": (at(2, True), r_l1.at[k], mate_device, 0),
            "mate right": (at(1, True), r_x.at[k, 0], right, 2),
            "mate left": (at(-1, True), r_x.at[k, 1], left, 4),
            "pass": (at(2, False), r_h.at[k], left if h else right, 6),
            "own right": (at(1, False), r_f.at[k, 0], right, 8),
            "own left": (at(-1, False), r_f.at[k, 1], left, 10),
            "own mate": (at(0, True), r_l2.at[k], mate_device, 12),
        }[kind]
        return remote(
            part.at[i, block, e, halves[h]], dst.at[halves[h]],
            s_send.at[k, index + h], s_recv.at[k, index + h], device,
        )

    def start(copy, s, *names):
        for name in names:
            made = copy(s, name)
            made.start()
            pending.append(made)

    def arrived(copy, s, *names):
        for name in names:
            copy(s, name).wait_recv()

    def own(s, h):
        sides = ("own left", "own mate", "own right") if h else ("own right", "own mate", "own left")
        start(gather_copy, s, *((side, h) for side in sides))

    def mate(s, h):
        arrived(gather_copy, s, ("own mate", h))
        start(gather_copy, s, ("mate right", h), ("mate left", h))

    def pass_on(s, h):
        arrived(gather_copy, s, ("own left" if h else "own right", h))
        start(gather_copy, s, ("pass", h))

    def diagonal(s, h):
        arrived(gather_copy, s, ("pass", h))
        start(gather_copy, s, ("diagonal", h))

    def experts(s):
        i, e = s
        while loads:
            loads.pop().wait()
        arrived(gather_copy, s, ("own right", 1), ("own left", 0))
        for h in range(2):
            arrived(gather_copy, s, ("mate right", h), ("mate left", h), ("diagonal", h))
        block = gath[i, :, e]
        lhs = block.reshape(block.shape[0] * block.shape[1], block.shape[2])
        hidden = gelu(jnp.dot(lhs, w1[e], preferred_element_type=F32)).astype(BF16)
        result = jnp.dot(hidden, w2[e], preferred_element_type=F32)
        part[i, :, e] = result.astype(BF16).reshape(block.shape)
        for h in (1, 0) if i else (0, 1):
            start(scatter_copy, s, ("diagonal mate", h), ("mate right", h), ("mate left", h))
        start(scatter_copy, s, ("own right", 1), ("own left", 0))

    def add(ref, *others):
        value = ref[...].astype(F32)
        for other in others:
            value = value + other.astype(F32)
        ref[...] = value.astype(BF16)

    def sum_diagonal(s, h):
        i, e = s
        arrived(scatter_copy, s, ("diagonal mate", h))
        add(part.at[i, at(2, False), e, halves[h]], r_l1[i * 2 + e, halves[h]])
        start(scatter_copy, s, ("pass", h))

    def sum_mate(s, h):
        i, e = s
        k = i * 2 + e
        arrived(scatter_copy, s, ("mate right", h), ("mate left", h))
        add(part.at[i, at(0, True), e, halves[h]], r_x[k, 0, halves[h]], r_x[k, 1, halves[h]])
        start(scatter_copy, s, ("own mate", h))

    def sum_half(s, h):
        i, e = s
        arrived(scatter_copy, s, ("pass", h))
        add(part.at[i, at(-1 if h else 1, False), e, halves[h]], r_h[i * 2 + e, halves[h]])
        start(scatter_copy, s, ("own left" if h else "own right", h))

    def sum_own(s, h):
        i, e = s
        k = i * 2 + e
        arrived(scatter_copy, s, ("own right", h), ("own left", h), ("own mate", h))
        value = part[i, n, e, halves[h]].astype(F32) + r_f[k, 0, halves[h]].astype(F32)
        value = value + r_f[k, 1, halves[h]].astype(F32) + r_l2[k, halves[h]].astype(F32)
        total[i, h, e] = value.astype(BF16)

    def give_back(i, h):
        both = total[i, h]
        both = both.reshape(2 * half, both.shape[2])
        rows[0:n_wide, :] = jnp.dot(order(half, True), both, preferred_element_type=F32)
        to_pairs(give2.at[i], h * half, half)
        to_all(give2.at[i], take2.at[i], 2 + i, h, False)

    def finish(i):
        for h in range(2):
            from_all(give2.at[i], take2.at[i], 2 + i, h, False)
        from_pairs(take2.at[i], 0, n_wide)
        res_ref[i] = jnp.dot(comb[i], rows[...].astype(BF16), preferred_element_type=F32).astype(BF16)

    steps = (
        dispatch, unpack, own, mate, pass_on, diagonal, experts,
        sum_diagonal, sum_mate, sum_half, sum_own, give_back, finish,
    )
    for name, *what in plan:
        steps[name](*what)

    for h in range(2):
        for i in range(2):
            all_sent(give.at[i], i, h)
            all_sent(give2.at[i], 2 + i, h)
    for copy in pending:
        copy.wait_send()


def per_device(n_wide, n_narrow, tokens, slot_params, expand_weight, reduce_weight):
    images, m, d = tokens.shape
    experts = slot_params.shape[0]
    rows = (n_wide, d)
    anyspace = pl.BlockSpec(memory_space=pl.ANY)
    dma = pltpu.SemaphoreType.DMA
    return pl.pallas_call(
        functools.partial(exchange_kernel, n_wide, PLAN),
        out_shape=pltpu.VMEM(tokens.shape, BF16),
        in_specs=[anyspace] * 4,
        out_specs=pl.BlockSpec(memory_space=pltpu.VMEM),
        scratch_shapes=[
            pltpu.VMEM(tokens.shape, BF16),
            pltpu.VMEM(slot_params.shape, BF16),
            pltpu.VMEM(expand_weight.shape, BF16),
            pltpu.VMEM(reduce_weight.shape, BF16),
            pltpu.VMEM((experts, d), F32),
            pltpu.VMEM((images, m, experts), BF16),
            pltpu.VMEM((2, n_wide, 2, d), BF16),
            pltpu.VMEM((2, n_wide, 2, d), BF16),
            pltpu.VMEM((2, n_narrow, 2, *rows), BF16),
            pltpu.VMEM((2, n_narrow, 2, *rows), BF16),
            pltpu.VMEM((4, *rows), BF16),
            pltpu.VMEM((4, 2, *rows), BF16),
            pltpu.VMEM((4, *rows), BF16),
            pltpu.VMEM((4, 2, *rows), BF16),
            pltpu.VMEM((4, *rows), BF16),
            pltpu.VMEM((2, 2, 2, n_wide // 2, d), BF16),
            pltpu.VMEM((2, n_wide, 2, d), BF16),
            pltpu.VMEM((2, n_wide, 2, d), BF16),
            dma((8,)), dma((4,)), dma((4, 2)), dma((4, 2)), dma((4, 14)), dma((4, 14)),
            dma((4, 14)), dma((4, 14)),
        ],
        compiler_params=pltpu.CompilerParams(
            collective_id=0, has_side_effects=True, vmem_limit_bytes=56 * 1024 * 1024
        ),
        name="exchange",
    )(tokens, slot_params, expand_weight, reduce_weight)


def solution(mesh):
    in_specs = (
        P(("wide", "narrow"), None, None),
        P(),
        P("wide", None, "narrow"),
        P("wide", "narrow", None),
    )
    return jax.shard_map(
        functools.partial(per_device, mesh.shape["wide"], mesh.shape["narrow"]),
        mesh=mesh,
        in_specs=in_specs,
        out_specs=P(("wide", "narrow"), None, None),
        check_vma=False,
    )
```

```python
import functools

import jax
import jax.numpy as jnp
from jax import lax
from jax.experimental import pallas as pl
from jax.experimental.pallas import tpu as pltpu
from jax.sharding import PartitionSpec as P

MESH = pl.DeviceIdType.MESH
NX = 4
NZ = 4
F32 = jnp.float32
BF16 = jnp.bfloat16

(
    DISPATCH, UNPACK, OWN, MATE, PASS, DIAGONAL, EXPERTS,
    SUM_DIAGONAL, SUM_MATE, SUM_HALF, SUM_OWN, GIVE_BACK, FINISH,
) = range(13)
PLAN = (
    (DISPATCH, 0), (DISPATCH, 1), (UNPACK, 0, 0), (OWN, (0, 0), 0), (OWN, (0, 1), 0), (UNPACK, 0, 1),
    (OWN, (0, 0), 1), (OWN, (0, 1), 1), (UNPACK, 1, 0), (MATE, (0, 0), 0), (PASS, (0, 0), 0), (OWN, (1, 1), 0),
    (OWN, (1, 0), 0), (PASS, (0, 1), 0), (MATE, (0, 1), 0), (UNPACK, 1, 1), (PASS, (0, 0), 1), (MATE, (0, 0), 1),
    (OWN, (1, 0), 1), (OWN, (1, 1), 1), (MATE, (0, 1), 1), (PASS, (0, 1), 1), (MATE, (1, 1), 0),
    (DIAGONAL, (0, 0), 0), (MATE, (1, 0), 0), (PASS, (1, 1), 0), (MATE, (1, 0), 1), (PASS, (1, 0), 0),
    (MATE, (1, 1), 1), (DIAGONAL, (0, 0), 1), (DIAGONAL, (0, 1), 0), (PASS, (1, 0), 1), (PASS, (1, 1), 1),
    (EXPERTS, (0, 0)), (DIAGONAL, (0, 1), 1), (DIAGONAL, (1, 1), 0), (SUM_DIAGONAL, (0, 0), 0),
    (DIAGONAL, (1, 0), 1), (DIAGONAL, (1, 0), 0), (SUM_DIAGONAL, (0, 0), 1), (DIAGONAL, (1, 1), 1),
    (EXPERTS, (0, 1)), (SUM_MATE, (0, 0), 1), (SUM_MATE, (0, 0), 0), (EXPERTS, (1, 0)), (SUM_HALF, (0, 0), 1),
    (SUM_HALF, (0, 0), 0), (SUM_DIAGONAL, (0, 1), 0), (EXPERTS, (1, 1)), (SUM_DIAGONAL, (0, 1), 1),
    (SUM_MATE, (0, 1), 1), (SUM_MATE, (0, 1), 0), (SUM_MATE, (1, 0), 1), (SUM_DIAGONAL, (1, 0), 1),
    (SUM_MATE, (1, 0), 0), (SUM_DIAGONAL, (1, 0), 0), (SUM_DIAGONAL, (1, 1), 1), (SUM_OWN, (0, 0), 0),
    (SUM_OWN, (0, 0), 1), (SUM_DIAGONAL, (1, 1), 0), (SUM_HALF, (0, 1), 0), (SUM_MATE, (1, 1), 1),
    (SUM_MATE, (1, 1), 0), (SUM_HALF, (0, 1), 1), (SUM_HALF, (1, 0), 1), (SUM_HALF, (1, 1), 1),
    (SUM_HALF, (1, 0), 0), (SUM_HALF, (1, 1), 0), (SUM_OWN, (0, 1), 0), (GIVE_BACK, 0, 0), (SUM_OWN, (0, 1), 1),
    (GIVE_BACK, 0, 1), (SUM_OWN, (1, 0), 1), (SUM_OWN, (1, 1), 1), (GIVE_BACK, 1, 1), (SUM_OWN, (1, 0), 0),
    (SUM_OWN, (1, 1), 0), (GIVE_BACK, 1, 0), (FINISH, 0), (FINISH, 1),
)


def gelu(v):
    return 0.5 * v * (1.0 + jnp.tanh(0.7978845608028654 * (v + 0.044715 * (v * v * v))))


def exchange_kernel(
    n_wide, plan,
    tok_hbm, slot_hbm, w1_hbm, w2_hbm,
    res_ref,
    tok, slot, w1, w2, rows, scores, comb, give, take, gath, part, r_l1, r_x, r_h, r_f, r_l2, total, give2, take2,
    load_sem, own_sem, a_send, a_recv, g_send, g_recv, s_send, s_recv,
):
    w, n = lax.axis_index("wide"), lax.axis_index("narrow")
    x, z = n // 2, lax.rem(n, 2)
    group = n_wide // NZ
    w_group, w_place = w // group, lax.rem(w, group)
    half = n_wide // 2
    halves = (pl.ds(0, half), pl.ds(half, half))
    pending = []

    def at(dx, other):
        zz = 1 - z if other else z
        return lax.rem(x + dx + NX, NX) * 2 + zz

    right, left, mate_device = (w, at(1, False)), (w, at(-1, False)), (w, at(0, True))

    quarter = tok.shape[1] // 4
    loads = [pltpu.make_async_copy(slot_hbm, slot, load_sem.at[0])]
    for k in range(4):
        rows_k = pl.ds(k * quarter, quarter)
        loads.append(pltpu.make_async_copy(tok_hbm.at[0, rows_k], tok.at[0, rows_k], load_sem.at[1 + k]))
    loads += [
        pltpu.make_async_copy(tok_hbm.at[1], tok.at[1], load_sem.at[5]),
        pltpu.make_async_copy(w1_hbm, w1, load_sem.at[6]),
        pltpu.make_async_copy(w2_hbm, w2, load_sem.at[7]),
    ]
    for load in loads[:6]:
        load.start()

    other = x * 2 + 1 - z
    near, away = 3 - 2 * z, 1 + 2 * z
    outward = (((0, n), (near, other)), ((away, n), (2, other)))
    homeward = (((0, n), (near, other)), ((near, n), (2, other)))

    barrier = pltpu.get_barrier_semaphore()

    for first, step, to_narrow in ((0, 2, other), (0, away, n), (0, near, n), (0, near, other), (1, 0, n)):
        to_group = lax.rem(w_group + step, NZ) * group

        @pl.loop(first, group)
        def _(q):
            to = to_group + lax.rem(w_place + q, group)
            pl.semaphore_signal(barrier, inc=1, device_id=(to, to_narrow), device_id_type=MESH)

    for device in (right, left, mate_device):
        pl.semaphore_signal(barrier, inc=1, device_id=device, device_id_type=MESH)

    def remote(src, dst, send, recv, device):
        return pltpu.make_async_remote_copy(
            src_ref=src, dst_ref=dst, send_sem=send, recv_sem=recv,
            device_id=device, device_id_type=MESH,
        )

    def to_all(src, dst, k, h, by_owner):
        for j in (1, 0):
            step, to_narrow = (outward if by_owner else homeward)[h][j]
            to_group = lax.rem(w_group + step, NZ) * group
            base = h * half + j * group

            @pl.loop(0 if h or j else 1, group)
            def _(q):
                place = lax.rem(w_place + q, group)
                to = to_group + place
                mine, theirs = (to, base + w_place) if by_owner else (base + place, w)
                remote(
                    src.at[mine], dst.at[theirs], a_send.at[k, h], a_recv.at[k, h], (to, to_narrow)
                ).start()

        if h == 0:
            own_copy(src, dst, k, by_owner).start()

    def own_copy(src, dst, k, by_owner):
        mine, theirs = (w, w_place) if by_owner else (w_place, w)
        return pltpu.make_async_copy(src.at[mine], dst.at[theirs], own_sem.at[k])

    def from_all(src, dst, k, h, by_owner):
        if h == 0:
            own_copy(src, dst, k, by_owner).wait()
        others = pl.ds(0, 2 * group - (h == 0))
        pltpu.make_async_copy(dst.at[others], dst.at[others], a_recv.at[k, h]).wait()

    def all_sent(src, k, h):
        others = pl.ds(0, 2 * group - (h == 0))
        pltpu.make_async_copy(src.at[others], src.at[others], a_send.at[k, h]).wait()

    def to_pairs(dst, first, count):
        for k in range(count):
            dst[first + k] = rows[2 * k : 2 * k + 2, :].astype(BF16)

    def from_pairs(src, first, count):
        for k in range(count):
            rows[2 * k : 2 * k + 2, :] = src[first + k].astype(F32)

    def order(count, back):
        shape = (2 * count, 2 * count)
        r, q = lax.broadcasted_iota(jnp.int32, shape, 0), lax.broadcasted_iota(jnp.int32, shape, 1)
        if back:
            r, q = q, r
        same = (r % count) * 2 + r // count == q
        return jnp.where(same, 1.0, 0.0).astype(BF16)

    def dispatch(i):
        for _ in range(1 if i else 5):
            loads.pop(0).wait()
        t = tok[i]
        logits = lax.dot_general(slot[...], t, (((1,), (1,)), ((), ())), preferred_element_type=F32)
        up = jnp.exp(logits - jnp.max(logits, axis=1, keepdims=True))
        weights = (up / jnp.sum(up, axis=1, keepdims=True)).astype(BF16)
        rows[...] = jnp.dot(weights, t, preferred_element_type=F32)
        to_pairs(give.at[i], 0, n_wide)
        if i == 0:
            pl.semaphore_wait(barrier, 5 * group - 1 + 3)
        for h in range(2):
            to_all(give.at[i], take.at[i], i, h, True)
        if i == 0:
            for load in loads[1:]:
                load.start()
        scores[i] = logits
        if i == 1:
            for j in range(2):
                logits = scores[j]
                up = jnp.exp(logits - jnp.max(logits, axis=0, keepdims=True))
                comb[j] = (up / jnp.sum(up, axis=0, keepdims=True)).T.astype(BF16)

    def unpack(i, h):
        from_all(give.at[i], take.at[i], i, h, True)
        from_pairs(take.at[i], h * half, half)
        some = rows[0:n_wide, :].astype(BF16)
        by_expert = jnp.dot(order(half, False), some, preferred_element_type=F32)
        gath[i, n, :, halves[h], :] = by_expert.astype(BF16).reshape(2, half, by_expert.shape[1])

    def gather_copy(s, name):
        i, e = s
        kind, h = name
        g = gath.at[i]
        block, device, index = {
            "own right": (n, right, 0),
            "own left": (n, left, 2),
            "own mate": (n, mate_device, 4),
            "mate right": (at(0, True), right, 6),
            "mate left": (at(0, True), left, 8),
            "pass": (at(1 if h else -1, False), left if h else right, 10),
            "diagonal": (at(2, False), mate_device, 12),
        }[kind]
        ref = g.at[block, e, halves[h]]
        return remote(ref, ref, g_send.at[i * 2 + e, index + h], g_recv.at[i * 2 + e, index + h], device)

    def scatter_copy(s, name):
        i, e = s
        k = i * 2 + e
        kind, h = name
        block, dst, device, index = {
            "diagonal mate": (at(2, True), r_l1.at[k], mate_device, 0),
            "mate right": (at(1, True), r_x.at[k, 0], right, 2),
            "mate left": (at(-1, True), r_x.at[k, 1], left, 4),
            "pass": (at(2, False), r_h.at[k], left if h else right, 6),
            "own right": (at(1, False), r_f.at[k, 0], right, 8),
            "own left": (at(-1, False), r_f.at[k, 1], left, 10),
            "own mate": (at(0, True), r_l2.at[k], mate_device, 12),
        }[kind]
        return remote(
            part.at[i, block, e, halves[h]], dst.at[halves[h]],
            s_send.at[k, index + h], s_recv.at[k, index + h], device,
        )

    def start(copy, s, *names):
        for name in names:
            made = copy(s, name)
            made.start()
            pending.append(made)

    def arrived(copy, s, *names):
        for name in names:
            copy(s, name).wait_recv()

    def own(s, h):
        sides = ("own mate", "own left", "own right") if h else ("own mate", "own right", "own left")
        start(gather_copy, s, *((side, h) for side in sides))

    def mate(s, h):
        arrived(gather_copy, s, ("own mate", h))
        start(gather_copy, s, ("mate right", h), ("mate left", h))

    def pass_on(s, h):
        arrived(gather_copy, s, ("own left" if h else "own right", h))
        start(gather_copy, s, ("pass", h))

    def diagonal(s, h):
        arrived(gather_copy, s, ("pass", h))
        start(gather_copy, s, ("diagonal", h))

    def experts(s):
        i, e = s
        while loads:
            loads.pop().wait()
        arrived(gather_copy, s, ("own right", 1), ("own left", 0))
        for h in range(2):
            arrived(gather_copy, s, ("mate right", h), ("mate left", h), ("diagonal", h))
        block = gath[i, :, e]
        lhs = block.reshape(block.shape[0] * block.shape[1], block.shape[2])
        hidden = gelu(jnp.dot(lhs, w1[e], preferred_element_type=F32)).astype(BF16)
        result = jnp.dot(hidden, w2[e], preferred_element_type=F32)
        part[i, :, e] = result.astype(BF16).reshape(block.shape)
        for h in (1, 0) if i else (0, 1):
            start(scatter_copy, s, ("diagonal mate", h), ("mate right", h), ("mate left", h))
        start(scatter_copy, s, ("own right", 1), ("own left", 0))

    def add(ref, *others):
        value = ref[...].astype(F32)
        for other in others:
            value = value + other.astype(F32)
        ref[...] = value.astype(BF16)

    def sum_diagonal(s, h):
        i, e = s
        arrived(scatter_copy, s, ("diagonal mate", h))
        add(part.at[i, at(2, False), e, halves[h]], r_l1[i * 2 + e, halves[h]])
        start(scatter_copy, s, ("pass", h))

    def sum_mate(s, h):
        i, e = s
        k = i * 2 + e
        arrived(scatter_copy, s, ("mate right", h), ("mate left", h))
        add(part.at[i, at(0, True), e, halves[h]], r_x[k, 0, halves[h]], r_x[k, 1, halves[h]])
        start(scatter_copy, s, ("own mate", h))

    def sum_half(s, h):
        i, e = s
        arrived(scatter_copy, s, ("pass", h))
        add(part.at[i, at(-1 if h else 1, False), e, halves[h]], r_h[i * 2 + e, halves[h]])
        start(scatter_copy, s, ("own left" if h else "own right", h))

    def sum_own(s, h):
        i, e = s
        k = i * 2 + e
        arrived(scatter_copy, s, ("own right", h), ("own left", h), ("own mate", h))
        value = part[i, n, e, halves[h]].astype(F32) + r_f[k, 0, halves[h]].astype(F32)
        value = value + r_f[k, 1, halves[h]].astype(F32) + r_l2[k, halves[h]].astype(F32)
        total[i, h, e] = value.astype(BF16)

    def give_back(i, h):
        both = total[i, h]
        both = both.reshape(2 * half, both.shape[2])
        rows[0:n_wide, :] = jnp.dot(order(half, True), both, preferred_element_type=F32)
        to_pairs(give2.at[i], h * half, half)
        to_all(give2.at[i], take2.at[i], 2 + i, h, False)

    def finish(i):
        for h in range(2):
            from_all(give2.at[i], take2.at[i], 2 + i, h, False)
        from_pairs(take2.at[i], 0, n_wide)
        res_ref[i] = jnp.dot(comb[i], rows[...].astype(BF16), preferred_element_type=F32).astype(BF16)

    steps = (
        dispatch, unpack, own, mate, pass_on, diagonal, experts,
        sum_diagonal, sum_mate, sum_half, sum_own, give_back, finish,
    )
    for name, *what in plan:
        steps[name](*what)

    for h in range(2):
        for i in range(2):
            all_sent(give.at[i], i, h)
            all_sent(give2.at[i], 2 + i, h)
    for copy in pending:
        copy.wait_send()


def per_device(n_wide, n_narrow, tokens, slot_params, expand_weight, reduce_weight):
    images, m, d = tokens.shape
    experts = slot_params.shape[0]
    rows = (n_wide, d)
    anyspace = pl.BlockSpec(memory_space=pl.ANY)
    dma = pltpu.SemaphoreType.DMA
    return pl.pallas_call(
        functools.partial(exchange_kernel, n_wide, PLAN),
        out_shape=pltpu.VMEM(tokens.shape, BF16),
        in_specs=[anyspace] * 4,
        out_specs=pl.BlockSpec(memory_space=pltpu.VMEM),
        scratch_shapes=[
            pltpu.VMEM(tokens.shape, BF16),
            pltpu.VMEM(slot_params.shape, BF16),
            pltpu.VMEM(expand_weight.shape, BF16),
            pltpu.VMEM(reduce_weight.shape, BF16),
            pltpu.VMEM((experts, d), F32),
            pltpu.VMEM((images, experts, m), F32),
            pltpu.VMEM((images, m, experts), BF16),
            pltpu.VMEM((2, n_wide, 2, d), BF16),
            pltpu.VMEM((2, n_wide, 2, d), BF16),
            pltpu.VMEM((2, n_narrow, 2, *rows), BF16),
            pltpu.VMEM((2, n_narrow, 2, *rows), BF16),
            pltpu.VMEM((4, *rows), BF16),
            pltpu.VMEM((4, 2, *rows), BF16),
            pltpu.VMEM((4, *rows), BF16),
            pltpu.VMEM((4, 2, *rows), BF16),
            pltpu.VMEM((4, *rows), BF16),
            pltpu.VMEM((2, 2, 2, n_wide // 2, d), BF16),
            pltpu.VMEM((2, n_wide, 2, d), BF16),
            pltpu.VMEM((2, n_wide, 2, d), BF16),
            dma((8,)), dma((4,)), dma((4, 2)), dma((4, 2)), dma((4, 14)), dma((4, 14)),
            dma((4, 14)), dma((4, 14)),
        ],
        compiler_params=pltpu.CompilerParams(
            collective_id=0, has_side_effects=True, vmem_limit_bytes=56 * 1024 * 1024
        ),
        name="exchange",
    )(tokens, slot_params, expand_weight, reduce_weight)


def solution(mesh):
    in_specs = (
        P(("wide", "narrow"), None, None),
        P(),
        P("wide", None, "narrow"),
        P("wide", "narrow", None),
    )
    return jax.shard_map(
        functools.partial(per_device, mesh.shape["wide"], mesh.shape["narrow"]),
        mesh=mesh,
        in_specs=in_specs,
        out_specs=P(("wide", "narrow"), None, None),
        check_vma=False,
    )
```
